512 devices in a mesh: outer: 8 (over x, z_lo), inner: 64 (over y, z_hi, core).
Axes of the slice: x: 4, y: 8, z: 8 (z_hi: 4, z_lo: 2; z = z_hi * 2 + z_lo), core: 2. Of those that a mesh axis runs over, the one named last changes fastest.
Arguments:
- queries: bfloat16 [131072, 1024], P(('outer', 'inner')), may hold values from -160 to 160
- key_rows: bfloat16 [131072, 128], P(('outer', 'inner')), may hold values from -4 to 4
- value_rows: bfloat16 [131072, 128], P(('outer', 'inner')), may hold values from -5 to 5
- grad_out: bfloat16 [131072, 1024], P(('outer', 'inner')), may hold values from -5 to 5
- doc_starts: int32 [341], replicated, may hold values from 0 to 131071, as said below
- doc_ids: int32 [131072], P(('outer', 'inner')), may hold values from 0 to 340, as said below
Outputs:
- attended: bfloat16 [131072, 1024], P(('outer', 'inner'))
- query_grad: bfloat16 [131072, 1024], P(('outer', 'inner'))
- key_grad: bfloat16 [131072, 128], P(('outer', 'inner'))
- value_grad: bfloat16 [131072, 128], P(('outer', 'inner'))
The draws below stay inside these ranges and needn't reach their ends.
Inputs may be any that keep to these rules, and one draw needn't show every extreme that they name: doc_starts[0] = 0 and the starts rise; each document runs up to the next start (the last to 131072); every document holds 1 to 767 tokens, and one holds exactly 767. doc_ids[t] is the document whose range holds position t.
All inputs are finite; a program needn't handle non-finite values.
Results may differ from the reference program's by a relative error of at most 0.028.
Values may be sent and summed in bfloat16 or wider, within the bound.
A program may use at most 64 MiB of HBM per device.

```python
import math
import jax
import jax.numpy as jnp
from jax import lax

TOK_DEV = 256
HEADS = 8
HEAD_DIM = 128
LEVELS = 2
TOKENS = 131072
DOCMAX = 767
NDOCS = 341


def shared_tables(key):
    base_keys = jnp.clip(jax.random.normal(jax.random.fold_in(key, 11), (TOKENS, HEAD_DIM), jnp.float32), -4.0, 4.0)
    odd_rows = jnp.arange(TOKENS) % 2 == 1
    chosen = (jax.random.randint(jax.random.fold_in(key, 12), (TOKENS,), 0, 32) == 0) & odd_rows
    marked = jnp.roll(chosen, -1)
    key_table = jnp.where(marked[:, None], base_keys, base_keys)
    return key_table


def document_layout(key):
    stride_len = (DOCMAX + 1) // 2
    doc_index = jnp.arange(NDOCS, dtype=jnp.int32)
    offsets_extra = jax.random.randint(jax.random.fold_in(key, 21), (NDOCS,), 0, stride_len)
    longest = jax.random.randint(jax.random.fold_in(key, 22), (), 0, NDOCS - 1)
    offsets_extra = jnp.where(doc_index == longest, 0, offsets_extra)
    offsets_extra = jnp.where(doc_index == longest + 1, stride_len - 1, offsets_extra)
    offsets_extra = jnp.where(doc_index == 0, 0, offsets_extra)
    starts = (doc_index * stride_len + offsets_extra).astype(jnp.int32)
    positions = jnp.arange(TOKENS, dtype=jnp.int32)
    owners = (jnp.searchsorted(starts, positions, side='right') - 1).astype(jnp.int32)
    return (starts, owners)


def draw_key_rows(key, part):
    key_table = shared_tables(key)
    return key_table.astype(jnp.bfloat16)


def draw_queries(key, part):
    key = jax.random.fold_in(key, 4)
    result = jnp.clip(jax.random.normal(jax.random.fold_in(key, 5), (TOKENS, HEADS, HEAD_DIM), jnp.float32), -4.0, 4.0)
    return jnp.clip(result, -160.0, 160.0).reshape(TOKENS, HEADS * HEAD_DIM).astype(jnp.bfloat16)


def draw_doc_starts(key, part):
    starts, owners = document_layout(key)
    return starts


def draw_doc_ids(key, part):
    starts, owners = document_layout(key)
    return owners


def shard_levels(rng, dims, cuts, smallest, largest):
    level = 1.0
    for dim, blocks in cuts:
        heights = jax.random.uniform(jax.random.fold_in(jax.random.fold_in(rng, 6), dim), (blocks,), jnp.float32, smallest / len(cuts), largest / len(cuts))
        level = level * jnp.repeat(jnp.exp(heights), dims[dim] // blocks).reshape((-1,) + (1,) * (len(dims) - 1 - dim))
    return level


def normal_values(rng, shape, width, limit, pieces=(), held_as=jnp.bfloat16):
    values = jax.random.normal(rng, shape, jnp.float32) * width
    if len(pieces) > 0:
        values = shard_levels(rng, shape, pieces, -0.22, 0.18) * values
    return jnp.clip(values, min=-limit, max=limit).astype(held_as)


def setup_inputs(seed: int = 0) -> dict:
    keys = jax.random.split(jax.random.key(seed), 7)
    return {
        "queries": draw_queries(jax.random.fold_in(keys[6], 71), 0),
        "key_rows": draw_key_rows(jax.random.fold_in(keys[6], 71), 0),
        "value_rows": normal_values(keys[2], (TOKENS, HEAD_DIM), 1.0, 5.0, ((0, 512),)),
        "grad_out": normal_values(keys[3], (TOKENS, HEADS * HEAD_DIM), 1.0, 5.0, ((0, 512),)),
        "doc_starts": draw_doc_starts(jax.random.fold_in(keys[6], 71), 0),
        "doc_ids": draw_doc_ids(jax.random.fold_in(keys[6], 71), 0),
    }


def reference(queries, key_rows, value_rows, grad_out, doc_starts, doc_ids):
    tok_count = TOK_DEV
    span_blocks = 2 ** LEVELS
    margin_rows = (span_blocks - 1) * tok_count
    window_rows = span_blocks * tok_count
    score_scale = 1.0 / math.sqrt(HEAD_DIM)
    padding = jnp.zeros((margin_rows, HEAD_DIM), jnp.bfloat16)
    keys_padded = jnp.concatenate([padding, key_rows], axis=0)
    values_padded = jnp.concatenate([padding, value_rows], axis=0)
    token_starts = jnp.take(doc_starts, doc_ids, axis=0).astype(jnp.int32)
    grad_init = jnp.zeros((TOKENS + margin_rows, HEAD_DIM), jnp.float32)

    def one_block(state_pair, block_number):
        key_grads, value_grads = state_pair
        first_row = (block_number * tok_count).astype(jnp.int32)
        query_block = lax.dynamic_slice_in_dim(queries, first_row, tok_count, 0).reshape(tok_count * HEADS, HEAD_DIM)
        grad_block = lax.dynamic_slice_in_dim(grad_out, first_row, tok_count, 0).reshape(tok_count * HEADS, HEAD_DIM)
        key_window = lax.dynamic_slice_in_dim(keys_padded, first_row, window_rows, 0)
        value_window = lax.dynamic_slice_in_dim(values_padded, first_row, window_rows, 0)
        key_positions = first_row - margin_rows + jnp.arange(window_rows, dtype=jnp.int32)
        query_positions = first_row + jnp.arange(tok_count, dtype=jnp.int32)
        query_starts = lax.dynamic_slice_in_dim(token_starts, first_row, tok_count, 0)
        allowed = (key_positions[None, :] >= query_starts[:, None]) & (key_positions[None, :] <= query_positions[:, None])
        scores = jnp.dot(query_block, key_window.T, preferred_element_type=jnp.float32) * score_scale
        scores = jnp.where(allowed[:, None, :], scores.reshape(tok_count, HEADS, window_rows), -jnp.inf)
        row_max = lax.optimization_barrier(jnp.max(scores, axis=-1))
        log_total = row_max + jnp.log(lax.optimization_barrier(jnp.sum(jnp.exp(scores - row_max[..., None]), axis=-1)))
        weights = jnp.exp(scores - log_total[..., None])
        weights_low = weights.astype(jnp.bfloat16).reshape(tok_count * HEADS, window_rows)
        attended = jnp.dot(weights_low, value_window, preferred_element_type=jnp.float32).astype(jnp.bfloat16)
        attended = lax.optimization_barrier(attended)
        delta_rows = lax.optimization_barrier(jnp.sum(grad_block.astype(jnp.float32) * attended.astype(jnp.float32), axis=-1)).reshape(tok_count, HEADS)
        grad_weights = jnp.dot(grad_block, value_window.T, preferred_element_type=jnp.float32).reshape(tok_count, HEADS, window_rows)
        grad_scores = (weights * (grad_weights - delta_rows[..., None]) * score_scale).astype(jnp.bfloat16)
        grad_scores = grad_scores.reshape(tok_count * HEADS, window_rows)
        query_grad = jnp.dot(grad_scores, key_window, preferred_element_type=jnp.float32).astype(jnp.bfloat16)
        key_part = jnp.dot(grad_scores.T, query_block, preferred_element_type=jnp.float32)
        value_part = jnp.dot(weights_low.T, grad_block, preferred_element_type=jnp.float32)
        key_grads = lax.dynamic_update_slice_in_dim(key_grads, lax.dynamic_slice_in_dim(key_grads, first_row, window_rows, 0) + key_part, first_row, 0)
        value_grads = lax.dynamic_update_slice_in_dim(value_grads, lax.dynamic_slice_in_dim(value_grads, first_row, window_rows, 0) + value_part, first_row, 0)
        return ((key_grads, value_grads), (attended.reshape(tok_count, HEADS * HEAD_DIM), query_grad.reshape(tok_count, HEADS * HEAD_DIM)))
    final_state, outputs = lax.scan(one_block, (grad_init, grad_init), jnp.arange(TOKENS // tok_count, dtype=jnp.int32))
    attended = outputs[0].reshape(TOKENS, HEADS * HEAD_DIM)
    query_grads = outputs[1].reshape(TOKENS, HEADS * HEAD_DIM)
    key_grad = final_state[0][margin_rows:].astype(jnp.bfloat16)
    value_grad = final_state[1][margin_rows:].astype(jnp.bfloat16)
    return (attended, query_grads, key_grad, value_grad)
```

```python
import functools
import math

import jax
import jax.numpy as jnp
from jax import lax
from jax.experimental import pallas as pl
from jax.experimental.pallas import tpu as pltpu
from jax.sharding import PartitionSpec as P

MESH = pl.DeviceIdType.MESH
SPAN = 4
CHUNK = 32
GROUP = 2
MASKED = -1e30
VMEM_BYTES = 48 * 2**20
F32 = jnp.float32
BF16 = jnp.bfloat16


def dot(left, right):
    return jnp.dot(left, right, preferred_element_type=F32)


def kernel(
    sizes,
    q_in, k_in, v_in, g_in, doc_in,
    att_out, dq_out, dk_out, dv_out,
    docs, q, g, qt, gt, kw, vw, kt, vt, bias, probs, dprobs, low, grad_low, row_max, row_sum, row_dot, block_max,
    relay_k, relay_v, part_k, part_v, send_k, send_v, got_k, got_v, att, dq, dk, dv,
    local_sem, out_sem, send_sem, recv_sem,
):
    outer_count, inner_count, tok, heads, dim = sizes
    total = outer_count * inner_count
    score_scale = 1.0 / math.sqrt(dim)
    to_log2 = score_scale * math.log2(math.e)
    me = lax.axis_index("outer") * inner_count + lax.axis_index("inner")
    odd = lax.rem(me, 2)

    def device(offset):
        place = lax.rem(me + offset + total, total)
        return (lax.div(place, inner_count), lax.rem(place, inner_count))

    sibling = device(1 - 2 * odd)

    has_two_before = me >= 2
    has_three_before = me >= 3
    has_two_after = me + 2 < total
    has_three_after = me + 3 < total
    is_odd = odd == 1
    is_even = odd == 0

    step = lax.div(lax.rem(me, 8), 2)
    relay = device(jnp.where(step == 0, 6, -2))
    relayed_from = device(jnp.where(step == 3, -6, 2))
    relay_target = jnp.where(step == 3, -3, 5)
    has_relay_target = me + relay_target < total
    relay_source = device(jnp.where(step == 2, 3, -5))

    for age in range(1, SPAN):

        @pl.when(me < age)
        def _(age=age):
            kw[age] = jnp.zeros_like(kw[age])
            vw[age] = jnp.zeros_like(vw[age])

    @pl.when(me + 3 >= total)
    def _():
        for slot in (0, 2):
            got_k[slot] = jnp.zeros_like(got_k[slot])
            got_v[slot] = jnp.zeros_like(got_v[slot])

    barrier = pltpu.get_barrier_semaphore()

    def greet(place):
        pl.semaphore_signal(barrier, inc=1, device_id=place, device_id_type=MESH)

    greet(sibling)

    @pl.when(has_two_before)
    def _():
        greet(device(-2))

    @pl.when(is_even & has_three_before)
    def _():
        greet(relay_source)

    @pl.when(is_odd & has_relay_target)
    def _():
        greet(relayed_from)

    key_load = pltpu.make_async_copy(k_in, kw.at[0], local_sem.at[0])
    value_load = pltpu.make_async_copy(v_in, vw.at[0], local_sem.at[1])
    doc_load = pltpu.make_async_copy(doc_in, docs, local_sem.at[2])
    head_loads = []
    for head in range(heads):
        here, there = pl.ds(head * dim, dim), pl.ds(head * tok, tok)
        head_loads += [
            pltpu.make_async_copy(q_in.at[:, here], q.at[there], local_sem.at[3 + head]),
            pltpu.make_async_copy(g_in.at[:, here], g.at[there], local_sem.at[3 + heads + head]),
        ]
    for copy in [key_load, value_load, doc_load] + head_loads:
        copy.start()

    def remote(source, target, place, number):
        return pltpu.make_async_remote_copy(
            src_ref=source,
            dst_ref=target,
            send_sem=send_sem.at[number],
            recv_sem=recv_sem.at[number],
            device_id=place,
            device_id_type=MESH,
        )

    def pair(keys, values, target_slot, place, number):
        return (
            remote(keys, kw.at[target_slot], place, number),
            remote(values, vw.at[target_slot], place, number + 1),
        )

    to_next = pair(kw.at[0], vw.at[0], 2, device(2), 0)
    own_to_sibling = pair(kw.at[0], vw.at[0], 1, sibling, 2)
    passed_to_sibling = pair(kw.at[2], vw.at[2], 1, sibling, 2)
    passed_on = pair(kw.at[2], vw.at[2], 3, sibling, 4)
    relay_in = (
        remote(kw.at[0], relay_k, relay, 12),
        remote(vw.at[0], relay_v, relay, 13),
    )
    relay_out = pair(relay_k, relay_v, 3, device(relay_target), 4)
    third = (
        remote(send_k.at[0], got_k.at[0], device(2 * odd - 3), 6),
        remote(send_v.at[0], got_v.at[0], device(2 * odd - 3), 7),
    )
    first = (
        remote(send_k.at[1], got_k.at[1], sibling, 8),
        remote(send_v.at[1], got_v.at[1], sibling, 9),
    )
    second = (
        remote(send_k.at[2], got_k.at[2], device(-2), 10),
        remote(send_v.at[2], got_v.at[2], device(-2), 11),
    )

    def start(copies):
        for copy in copies:
            copy.start()

    def received(copies):
        for copy in copies:
            copy.wait_recv()

    def sent(copies):
        for copy in copies:
            copy.wait_send()

    key_load.wait()
    value_load.wait()
    targets = 1 + jnp.where(has_two_after, 1, 0)
    targets += jnp.where(is_odd & has_three_after, 1, 0)
    targets += jnp.where(is_odd & has_relay_target, 1, 0)
    pl.semaphore_wait(barrier, targets)

    @pl.when(is_even)
    def _():
        start(own_to_sibling)

    @pl.when(is_odd & has_two_after)
    def _():
        start(to_next)

    @pl.when(is_odd & has_three_after)
    def _():
        start(relay_in)

    doc_load.wait()
    first_row = (me * tok).astype(F32)
    doc_starts = jnp.broadcast_to(docs[...][None, :].astype(F32), (tok, docs.shape[0])) - first_row
    positions = lax.broadcasted_iota(jnp.int32, doc_starts.shape, 0).astype(F32)
    starts = jnp.max(
        jnp.where(doc_starts <= positions, doc_starts, -first_row), axis=1, keepdims=True
    )
    starts = jnp.broadcast_to(starts, (tok, dim)).T[:1]
    places = lax.broadcasted_iota(jnp.int32, (tok, tok), 0)
    for age in range(SPAN):
        allowed = (places - age * tok).astype(F32) >= starts
        if age == 0:
            allowed = allowed & (places <= lax.broadcasted_iota(jnp.int32, (tok, tok), 1))
        bias[age] = jnp.where(allowed, 0.0, MASKED)

    def of_head(head, count=1):
        return slice(head * tok, (head + count) * tok)

    for copy in head_loads:
        copy.wait()
    for head in range(heads):
        qt[head] = q[of_head(head)].T
        gt[head] = g[of_head(head)].T

    def turn(slot):
        kt[:, of_head(slot)] = kw[slot].T
        vt[:, of_head(slot)] = vw[slot].T

    def folded(values, combine):
        return combine(values.reshape(-1, 8, tok), axis=0)

    def multiply(slot, head, fresh):
        scores = dot(kw[slot], qt[head]) + bias[slot]
        probs[slot, head] = scores
        top = jnp.max(folded(scores, jnp.max), axis=0, keepdims=True)
        if not fresh:
            top = jnp.maximum(row_max[head], top)
        dprobs[slot, head] = dot(vw[slot], gt[head])
        block_max[slot, head] = top

    def weigh(slot, head, fresh):
        top = block_max[slot, head]
        added = jnp.zeros((8, tok), F32)
        dotted = jnp.zeros((8, tok), F32)
        for row in range(0, tok, CHUNK):
            rows = slice(row, row + CHUNK)
            weights = jnp.exp2((probs[slot, head, rows] - top) * to_log2)
            probs[slot, head, rows] = weights
            added += folded(weights, jnp.sum)
            dotted += folded(weights * dprobs[slot, head, rows], jnp.sum)
        added = jnp.sum(added, axis=0, keepdims=True)
        dotted = jnp.sum(dotted, axis=0, keepdims=True)
        if not fresh:
            shrink = jnp.exp2((row_max[head] - top) * to_log2)
            added += row_sum[head] * shrink
            dotted += row_dot[head] * shrink
        row_max[head] = top
        row_sum[head] = added
        row_dot[head] = dotted

    def forward(slot, fresh):
        multiply(slot, 0, fresh)
        for head in range(heads):
            if head + 1 < heads:
                multiply(slot, head + 1, fresh)
            weigh(slot, head, fresh)

    def grade(slot, head):
        whole = 1.0 / row_sum[head]
        delta = row_dot[head] * whole
        scale = jnp.exp2((block_max[slot, head] - row_max[head]) * to_log2) * whole
        for row in range(0, tok, CHUNK):
            rows = slice(row, row + CHUNK)
            there = slice(slot * tok + row, slot * tok + row + CHUNK)
            weights = probs[slot, head, rows] * scale
            low[head, there] = weights.astype(BF16)
            grad_low[head, there] = (weights * (dprobs[slot, head, rows] - delta)).astype(BF16)

    def backward(slot):
        key_sum, value_sum = None, None
        for head in range(GROUP):
            grade(slot, head)
        for first_head in range(0, heads, GROUP):
            group = range(first_head, first_head + GROUP)
            if first_head + GROUP < heads:
                for head in group:
                    grade(slot, head + GROUP)
            side_by_side = [
                jnp.concatenate([ref[head, of_head(slot)] for head in group], axis=1)
                for ref in (grad_low, low)
            ]
            key_part = dot(side_by_side[0], q[of_head(first_head, GROUP)])
            value_part = dot(side_by_side[1], g[of_head(first_head, GROUP)])
            key_sum = key_part if key_sum is None else key_sum + key_part
            value_sum = value_part if value_sum is None else value_sum + value_part
        return key_sum, value_sum

    forward(0, True)

    @pl.when(is_odd & has_relay_target)
    def _():
        for arrived, onward in zip(relay_in, relay_out):
            arrived.wait_recv()
            onward.start()

    @pl.when(is_odd & has_two_before)
    def _():
        for arrived, onward in zip(to_next, passed_to_sibling):
            arrived.wait_recv()
            onward.start()

    @pl.when(is_even & has_two_after)
    def _():
        start(to_next)

    @pl.when(is_odd | has_two_before)
    def _():
        received(own_to_sibling)

    forward(1, False)

    @pl.when(is_even & has_two_before)
    def _():
        received(to_next)
        start(passed_on)

    forward(2, False)

    @pl.when(has_three_before)
    def _():
        received(relay_out)

    forward(3, False)
    key_sum, value_sum = backward(3)
    send_k[0] = key_sum.astype(BF16)
    send_v[0] = value_sum.astype(BF16)

    @pl.when(has_three_before)
    def _():
        start(third)

    key_sum, value_sum = backward(1)
    send_k[1] = key_sum.astype(BF16)
    send_v[1] = value_sum.astype(BF16)

    @pl.when(is_odd | has_two_before)
    def _():
        start(first)

    part_k[1], part_v[1] = backward(2)

    @pl.when(has_two_before)
    def _():
        @pl.when(is_odd)
        def _():
            received(first)

        @pl.when(is_even)
        def _():
            received(third)

        send_k[2] = (part_k[1] + got_k[odd].astype(F32)).astype(BF16)
        send_v[2] = (part_v[1] + got_v[odd].astype(F32)).astype(BF16)
        start(second)

    part_k[0], part_v[0] = backward(0)
    for slot in range(SPAN):
        turn(slot)
    for head in range(heads):
        columns = slice(head * dim, (head + 1) * dim)
        att[:, columns] = dot(vt[...], low[head]).T.astype(BF16)
        dq[:, columns] = (dot(kt[...], grad_low[head]) * score_scale).T.astype(BF16)
    att_copy = pltpu.make_async_copy(att, att_out, out_sem.at[0])
    att_copy.start()
    dq_copy = pltpu.make_async_copy(dq, dq_out, out_sem.at[1])
    dq_copy.start()

    @pl.when(is_even)
    def _():
        received(first)

    @pl.when(is_odd & has_three_after)
    def _():
        received(third)

    part_k[0] += got_k[1 - odd].astype(F32)
    part_v[0] += got_v[1 - odd].astype(F32)

    @pl.when(has_two_after)
    def _():
        received(second)

    dk[...] = ((part_k[0] + got_k[2].astype(F32)) * score_scale).astype(BF16)
    dk_copy = pltpu.make_async_copy(dk, dk_out, out_sem.at[2])
    dk_copy.start()
    dv[...] = (part_v[0] + got_v[2].astype(F32)).astype(BF16)
    dv_copy = pltpu.make_async_copy(dv, dv_out, out_sem.at[3])
    dv_copy.start()

    @pl.when(has_two_after)
    def _():
        sent(to_next)

    @pl.when(is_even | has_two_before)
    def _():
        sent(own_to_sibling)

    @pl.when(is_even & has_two_before)
    def _():
        sent(passed_on)

    @pl.when(is_odd & has_three_after)
    def _():
        sent(relay_in)

    @pl.when(is_odd & has_relay_target)
    def _():
        sent(relay_out)

    @pl.when(has_three_before)
    def _():
        sent(third)

    @pl.when(is_odd | has_two_before)
    def _():
        sent(first)

    @pl.when(has_two_before)
    def _():
        sent(second)

    for copy in (att_copy, dq_copy, dk_copy, dv_copy):
        copy.wait()


def write_out(*refs):
    count = (len(refs) - 1) // 2
    sems = refs[-1]
    copies = [
        pltpu.make_async_copy(refs[i], refs[count + i], sems.at[i]) for i in range(count)
    ]
    for copy in copies:
        copy.start()
    for copy in copies:
        copy.wait()


def local(sizes, queries, key_rows, value_rows, grad_out, doc_starts, doc_ids):
    outer_count, inner_count, tok, heads, dim = sizes
    width = heads * dim
    anywhere = pl.BlockSpec(memory_space=pl.ANY)
    row = (heads, 1, tok)
    shapes = (
        jax.ShapeDtypeStruct((tok, width), BF16),
        jax.ShapeDtypeStruct((tok, width), BF16),
        jax.ShapeDtypeStruct((tok, dim), BF16),
        jax.ShapeDtypeStruct((tok, dim), BF16),
    )
    in_hbm = [
        pltpu.with_memory_space_constraint(x, pltpu.HBM)
        for x in (queries, key_rows, value_rows, grad_out, doc_starts)
    ]
    results = pl.pallas_call(
        functools.partial(kernel, sizes),
        out_shape=tuple(pltpu.VMEM(shape.shape, shape.dtype) for shape in shapes),
        in_specs=[pl.BlockSpec(memory_space=pltpu.HBM)] * 5,
        out_specs=(anywhere,) * 4,
        scratch_shapes=[
            pltpu.VMEM(doc_starts.shape, jnp.int32),
            pltpu.VMEM((heads * tok, dim), BF16),
            pltpu.VMEM((heads * tok, dim), BF16),
            pltpu.VMEM((heads, dim, tok), BF16),
            pltpu.VMEM((heads, dim, tok), BF16),
            pltpu.VMEM((SPAN, tok, dim), BF16),
            pltpu.VMEM((SPAN, tok, dim), BF16),
            pltpu.VMEM((dim, SPAN * tok), BF16),
            pltpu.VMEM((dim, SPAN * tok), BF16),
            pltpu.VMEM((SPAN, tok, tok), F32),
            pltpu.VMEM((SPAN, heads, tok, tok), F32),
            pltpu.VMEM((SPAN, heads, tok, tok), F32),
            pltpu.VMEM((heads, SPAN * tok, tok), BF16),
            pltpu.VMEM((heads, SPAN * tok, tok), BF16),
            pltpu.VMEM(row, F32),
            pltpu.VMEM(row, F32),
            pltpu.VMEM(row, F32),
            pltpu.VMEM((SPAN,) + row, F32),
            pltpu.VMEM((tok, dim), BF16),
            pltpu.VMEM((tok, dim), BF16),
            pltpu.VMEM((2, tok, dim), F32),
            pltpu.VMEM((2, tok, dim), F32),
            pltpu.VMEM((SPAN - 1, tok, dim), BF16),
            pltpu.VMEM((SPAN - 1, tok, dim), BF16),
            pltpu.VMEM((SPAN - 1, tok, dim), BF16),
            pltpu.VMEM((SPAN - 1, tok, dim), BF16),
            pltpu.VMEM((tok, width), BF16),
            pltpu.VMEM((tok, width), BF16),
            pltpu.VMEM((tok, dim), BF16),
            pltpu.VMEM((tok, dim), BF16),
            pltpu.SemaphoreType.DMA((3 + 2 * heads,)),
            pltpu.SemaphoreType.DMA((4,)),
            pltpu.SemaphoreType.DMA((14,)),
            pltpu.SemaphoreType.DMA((14,)),
        ],
        compiler_params=pltpu.CompilerParams(
            collective_id=0, has_side_effects=True, vmem_limit_bytes=VMEM_BYTES
        ),
        cost_estimate=pl.CostEstimate(
            flops=12 * tok * heads * SPAN * tok * dim,
            bytes_accessed=8 * tok * (width + dim),
            transcendentals=SPAN * tok * tok * heads,
        ),
    )(*in_hbm)
    return pl.pallas_call(
        write_out,
        out_shape=shapes,
        in_specs=[anywhere] * 4,
        out_specs=(anywhere,) * 4,
        scratch_shapes=[pltpu.SemaphoreType.DMA((4,))],
        compiler_params=pltpu.CompilerParams(vmem_limit_bytes=VMEM_BYTES),
    )(*results)


def solution(mesh):
    rows = P(("outer", "inner"), None)

    def program(queries, key_rows, value_rows, grad_out, doc_starts, doc_ids):
        outer_count, inner_count = mesh.shape["outer"], mesh.shape["inner"]
        dim = key_rows.shape[1]
        sizes = (
            outer_count,
            inner_count,
            key_rows.shape[0] // (outer_count * inner_count),
            queries.shape[1] // dim,
            dim,
        )
        return jax.shard_map(
            functools.partial(local, sizes),
            mesh=mesh,
            in_specs=(rows, rows, rows, rows, P(), P(("outer", "inner"))),
            out_specs=(rows, rows, rows, rows),
            check_vma=False,
        )(queries, key_rows, value_rows, grad_out, doc_starts, doc_ids)

    return program
```

```python
import functools
import math

import jax
import jax.numpy as jnp
from jax import lax
from jax.experimental import pallas as pl
from jax.experimental.pallas import tpu as pltpu
from jax.sharding import PartitionSpec as P

MESH = pl.DeviceIdType.MESH
SPAN = 4
CHUNK = 32
GROUP = 2
UNROLL = 4
MASKED = -1e30
VMEM_BYTES = 48 * 2**20
F32 = jnp.float32
BF16 = jnp.bfloat16


def dot(left, right):
    return jnp.dot(left, right, preferred_element_type=F32)


def kernel(
    sizes,
    q_in, k_in, v_in, g_in, doc_in,
    att_out, dq_out, dk_out, dv_out,
    docs, q, g, qt, gt, kw, vw, kt, vt, bias, probs, dprobs, low, grad_low, row_max, row_sum, row_dot, block_max,
    relay_k, relay_v, key_sum, value_sum, send_k, send_v, got_k, got_v, att, dq, dk, dv,
    local_sem, out_sem, send_sem, recv_sem,
):
    outer_count, inner_count, tok, heads, dim = sizes
    total = outer_count * inner_count
    score_scale = 1.0 / math.sqrt(dim)
    to_log2 = score_scale * math.log2(math.e)
    me = lax.axis_index("outer") * inner_count + lax.axis_index("inner")
    odd = lax.rem(me, 2)

    def device(offset):
        place = lax.rem(me + offset + total, total)
        return (lax.div(place, inner_count), lax.rem(place, inner_count))

    sibling = device(1 - 2 * odd)

    has_two_before = me >= 2
    has_three_before = me >= 3
    has_two_after = me + 2 < total
    has_three_after = me + 3 < total
    is_odd = odd == 1
    is_even = odd == 0

    step = lax.div(lax.rem(me, 8), 2)
    relay = device(jnp.where(step == 0, 6, -2))
    relayed_from = device(jnp.where(step == 3, -6, 2))
    relay_target = jnp.where(step == 3, -3, 5)
    has_relay_target = me + relay_target < total
    relay_source = device(jnp.where(step == 2, 3, -5))

    for age in range(1, SPAN):

        @pl.when(me < age)
        def _(age=age):
            kw[age] = jnp.zeros_like(kw[age])
            vw[age] = jnp.zeros_like(vw[age])

    @pl.when(me + 3 >= total)
    def _():
        for slot in (0, 2):
            got_k[slot] = jnp.zeros_like(got_k[slot])
            got_v[slot] = jnp.zeros_like(got_v[slot])

    barrier = pltpu.get_barrier_semaphore()

    def greet(place):
        pl.semaphore_signal(barrier, inc=1, device_id=place, device_id_type=MESH)

    greet(sibling)

    @pl.when(has_two_before)
    def _():
        greet(device(-2))

    @pl.when(is_even & has_three_before)
    def _():
        greet(relay_source)

    @pl.when(is_odd & has_relay_target)
    def _():
        greet(relayed_from)

    key_load = pltpu.make_async_copy(k_in, kw.at[0], local_sem.at[0])
    value_load = pltpu.make_async_copy(v_in, vw.at[0], local_sem.at[1])
    doc_load = pltpu.make_async_copy(doc_in, docs, local_sem.at[2])
    head_loads = []
    for head in range(heads):
        here, there = pl.ds(head * dim, dim), pl.ds(head * tok, tok)
        head_loads += [
            pltpu.make_async_copy(q_in.at[:, here], q.at[there], local_sem.at[3 + head]),
            pltpu.make_async_copy(g_in.at[:, here], g.at[there], local_sem.at[3 + heads + head]),
        ]
    for copy in [key_load, value_load, doc_load] + head_loads:
        copy.start()

    def remote(source, target, place, number):
        return pltpu.make_async_remote_copy(
            src_ref=source,
            dst_ref=target,
            send_sem=send_sem.at[number],
            recv_sem=recv_sem.at[number],
            device_id=place,
            device_id_type=MESH,
        )

    def pair(keys, values, target_slot, place, number):
        return (
            remote(keys, kw.at[target_slot], place, number),
            remote(values, vw.at[target_slot], place, number + 1),
        )

    to_next = pair(kw.at[0], vw.at[0], 2, device(2), 0)
    own_to_sibling = pair(kw.at[0], vw.at[0], 1, sibling, 2)
    passed_to_sibling = pair(kw.at[2], vw.at[2], 1, sibling, 2)
    passed_on = pair(kw.at[2], vw.at[2], 3, sibling, 4)
    relay_in = (
        remote(kw.at[0], relay_k, relay, 12),
        remote(vw.at[0], relay_v, relay, 13),
    )
    relay_out = pair(relay_k, relay_v, 3, device(relay_target), 4)
    third = (
        remote(send_k.at[0], got_k.at[0], device(2 * odd - 3), 6),
        remote(send_v.at[0], got_v.at[0], device(2 * odd - 3), 7),
    )
    first = (
        remote(send_k.at[1], got_k.at[1], sibling, 8),
        remote(send_v.at[1], got_v.at[1], sibling, 9),
    )
    second = (
        remote(send_k.at[2], got_k.at[2], device(-2), 10),
        remote(send_v.at[2], got_v.at[2], device(-2), 11),
    )

    def start(copies):
        for copy in copies:
            copy.start()

    def received(copies):
        for copy in copies:
            copy.wait_recv()

    def sent(copies):
        for copy in copies:
            copy.wait_send()

    key_load.wait()
    value_load.wait()
    targets = 1 + jnp.where(has_two_after, 1, 0)
    targets += jnp.where(is_odd & has_three_after, 1, 0)
    targets += jnp.where(is_odd & has_relay_target, 1, 0)
    pl.semaphore_wait(barrier, targets)

    @pl.when(is_even)
    def _():
        start(own_to_sibling)

    @pl.when(is_odd & has_two_after)
    def _():
        start(to_next)

    @pl.when(is_odd & has_three_after)
    def _():
        start(relay_in)

    doc_load.wait()
    first_row = (me * tok).astype(F32)
    doc_starts = jnp.broadcast_to(docs[...][None, :].astype(F32), (tok, docs.shape[0])) - first_row
    positions = lax.broadcasted_iota(jnp.int32, doc_starts.shape, 0).astype(F32)
    starts = jnp.max(
        jnp.where(doc_starts <= positions, doc_starts, -first_row), axis=1, keepdims=True
    )
    starts = jnp.broadcast_to(starts, (tok, dim)).T[:1]
    places = lax.broadcasted_iota(jnp.int32, (tok, tok), 0)
    for age in range(SPAN):
        allowed = (places - age * tok).astype(F32) >= starts
        if age == 0:
            allowed = allowed & (places <= lax.broadcasted_iota(jnp.int32, (tok, tok), 1))
        bias[age] = jnp.where(allowed, 0.0, MASKED)

    def of_head(head, count=1):
        return pl.ds(pl.multiple_of(head * tok, tok), count * tok)

    for copy in head_loads:
        copy.wait()

    @pl.loop(0, heads // UNROLL)
    def _(part):
        for offset in range(UNROLL):
            head = part * UNROLL + offset
            qt[head] = q[of_head(head)].T
            gt[head] = g[of_head(head)].T

    row_max[...] = jnp.full_like(row_max, MASKED)
    row_sum[...] = jnp.zeros_like(row_sum)
    row_dot[...] = jnp.zeros_like(row_dot)

    def folded(values, combine):
        return combine(values.reshape(-1, 8, tok), axis=0)

    def multiply(slot, head):
        scores = dot(kw[slot], qt[head]) + bias[slot]
        probs[slot, head] = scores
        top = jnp.max(folded(scores, jnp.max), axis=0, keepdims=True)
        dprobs[slot, head] = dot(vw[slot], gt[head])
        block_max[slot, head] = jnp.maximum(row_max[head], top)

    def weigh(slot, head):
        top = block_max[slot, head]
        added = jnp.zeros((8, tok), F32)
        dotted = jnp.zeros((8, tok), F32)
        for row in range(0, tok, CHUNK):
            rows = slice(row, row + CHUNK)
            weights = jnp.exp2((probs[slot, head, rows] - top) * to_log2)
            probs[slot, head, rows] = weights
            added += folded(weights, jnp.sum)
            dotted += folded(weights * dprobs[slot, head, rows], jnp.sum)
        shrink = jnp.exp2((row_max[head] - top) * to_log2)
        row_max[head] = top
        row_sum[head] = row_sum[head] * shrink + jnp.sum(added, axis=0, keepdims=True)
        row_dot[head] = row_dot[head] * shrink + jnp.sum(dotted, axis=0, keepdims=True)

    def grade(slot, head):
        whole = 1.0 / row_sum[head]
        delta = row_dot[head] * whole
        scale = jnp.exp2((block_max[slot, head] - row_max[head]) * to_log2) * whole
        for row in range(0, tok, CHUNK):
            rows = slice(row, row + CHUNK)
            weights = probs[slot, head, rows] * scale
            low[head, slot, rows] = weights.astype(BF16)
            grad_low[head, slot, rows] = (
                weights * (dprobs[slot, head, rows] - delta)
            ).astype(BF16)

    @pl.loop(0, SPAN)
    def _(slot):
        @pl.when(slot == 1)
        def _():
            @pl.when(is_odd & has_relay_target)
            def _():
                for arrived, onward in zip(relay_in, relay_out):
                    arrived.wait_recv()
                    onward.start()

            @pl.when(is_odd & has_two_before)
            def _():
                for arrived, onward in zip(to_next, passed_to_sibling):
                    arrived.wait_recv()
                    onward.start()

            @pl.when(is_even & has_two_after)
            def _():
                start(to_next)

            @pl.when(is_odd | has_two_before)
            def _():
                received(own_to_sibling)

        @pl.when((slot == 2) & is_even & has_two_before)
        def _():
            received(to_next)
            start(passed_on)

        @pl.when((slot == 3) & has_three_before)
        def _():
            received(relay_out)

        @pl.loop(0, heads // UNROLL)
        def _(part):
            group = [part * UNROLL + offset for offset in range(UNROLL)]
            multiply(slot, group[0])
            for place, head in enumerate(group):
                if place + 1 < UNROLL:
                    multiply(slot, group[place + 1])
                weigh(slot, head)

    @pl.loop(0, SPAN)
    def _(turn):
        slot = jnp.where(turn == 0, 3, jnp.where(turn == 3, 0, turn))
        key_sum[...] = jnp.zeros_like(key_sum)
        value_sum[...] = jnp.zeros_like(value_sum)

        @pl.loop(0, heads // UNROLL)
        def _(part):
            keys, values = key_sum[...], value_sum[...]
            for pair_place in range(0, UNROLL, GROUP):
                first_head = part * UNROLL + pair_place
                group = [first_head + offset for offset in range(GROUP)]
                for head in group:
                    grade(slot, head)
                side_by_side = [
                    jnp.concatenate([ref[head, slot] for head in group], axis=1)
                    for ref in (grad_low, low)
                ]
                keys += dot(side_by_side[0], q[of_head(first_head, GROUP)])
                values += dot(side_by_side[1], g[of_head(first_head, GROUP)])
            key_sum[...] = keys
            value_sum[...] = values

        @pl.when((turn == 0) & has_three_before)
        def _():
            send_k[0] = key_sum[...].astype(BF16)
            send_v[0] = value_sum[...].astype(BF16)
            start(third)

        @pl.when((turn == 1) & (is_odd | has_two_before))
        def _():
            send_k[1] = key_sum[...].astype(BF16)
            send_v[1] = value_sum[...].astype(BF16)
            start(first)

        @pl.when((turn == 2) & has_two_before)
        def _():
            @pl.when(is_odd)
            def _():
                received(first)

            @pl.when(is_even)
            def _():
                received(third)

            send_k[2] = (key_sum[...] + got_k[odd].astype(F32)).astype(BF16)
            send_v[2] = (value_sum[...] + got_v[odd].astype(F32)).astype(BF16)
            start(second)

    for slot in range(SPAN):
        columns = slice(slot * tok, (slot + 1) * tok)
        kt[:, columns] = kw[slot].T
        vt[:, columns] = vw[slot].T

    @pl.loop(0, heads // GROUP)
    def _(part):
        for offset in range(GROUP):
            head = part * GROUP + offset
            columns = pl.ds(pl.multiple_of(head * dim, dim), dim)
            weights = low[head].reshape(SPAN * tok, tok)
            grads = grad_low[head].reshape(SPAN * tok, tok)
            att[:, columns] = dot(vt[...], weights).T.astype(BF16)
            dq[:, columns] = (dot(kt[...], grads) * score_scale).T.astype(BF16)

    att_copy = pltpu.make_async_copy(att, att_out, out_sem.at[0])
    att_copy.start()
    dq_copy = pltpu.make_async_copy(dq, dq_out, out_sem.at[1])
    dq_copy.start()

    @pl.when(is_even)
    def _():
        received(first)

    @pl.when(is_odd & has_three_after)
    def _():
        received(third)

    key_sum[...] += got_k[1 - odd].astype(F32)
    value_sum[...] += got_v[1 - odd].astype(F32)

    @pl.when(has_two_after)
    def _():
        received(second)

    dk[...] = ((key_sum[...] + got_k[2].astype(F32)) * score_scale).astype(BF16)
    dk_copy = pltpu.make_async_copy(dk, dk_out, out_sem.at[2])
    dk_copy.start()
    dv[...] = (value_sum[...] + got_v[2].astype(F32)).astype(BF16)
    dv_copy = pltpu.make_async_copy(dv, dv_out, out_sem.at[3])
    dv_copy.start()

    @pl.when(has_two_after)
    def _():
        sent(to_next)

    @pl.when(is_even | has_two_before)
    def _():
        sent(own_to_sibling)

    @pl.when(is_even & has_two_before)
    def _():
        sent(passed_on)

    @pl.when(is_odd & has_three_after)
    def _():
        sent(relay_in)

    @pl.when(is_odd & has_relay_target)
    def _():
        sent(relay_out)

    @pl.when(has_three_before)
    def _():
        sent(third)

    @pl.when(is_odd | has_two_before)
    def _():
        sent(first)

    @pl.when(has_two_before)
    def _():
        sent(second)

    for copy in (att_copy, dq_copy, dk_copy, dv_copy):
        copy.wait()


def write_out(*refs):
    count = (len(refs) - 1) // 2
    sems = refs[-1]
    copies = [
        pltpu.make_async_copy(refs[i], refs[count + i], sems.at[i]) for i in range(count)
    ]
    for copy in copies:
        copy.start()
    for copy in copies:
        copy.wait()


def local(sizes, queries, key_rows, value_rows, grad_out, doc_starts, doc_ids):
    outer_count, inner_count, tok, heads, dim = sizes
    width = heads * dim
    anywhere = pl.BlockSpec(memory_space=pl.ANY)
    row = (heads, 1, tok)
    shapes = (
        jax.ShapeDtypeStruct((tok, width), BF16),
        jax.ShapeDtypeStruct((tok, width), BF16),
        jax.ShapeDtypeStruct((tok, dim), BF16),
        jax.ShapeDtypeStruct((tok, dim), BF16),
    )
    in_hbm = [
        pltpu.with_memory_space_constraint(x, pltpu.HBM)
        for x in (queries, key_rows, value_rows, grad_out, doc_starts)
    ]
    results = pl.pallas_call(
        functools.partial(kernel, sizes),
        out_shape=tuple(pltpu.VMEM(shape.shape, shape.dtype) for shape in shapes),
        in_specs=[pl.BlockSpec(memory_space=pltpu.HBM)] * 5,
        out_specs=(anywhere,) * 4,
        scratch_shapes=[
            pltpu.VMEM(doc_starts.shape, jnp.int32),
            pltpu.VMEM((heads * tok, dim), BF16),
            pltpu.VMEM((heads * tok, dim), BF16),
            pltpu.VMEM((heads, dim, tok), BF16),
            pltpu.VMEM((heads, dim, tok), BF16),
            pltpu.VMEM((SPAN, tok, dim), BF16),
            pltpu.VMEM((SPAN, tok, dim), BF16),
            pltpu.VMEM((dim, SPAN * tok), BF16),
            pltpu.VMEM((dim, SPAN * tok), BF16),
            pltpu.VMEM((SPAN, tok, tok), F32),
            pltpu.VMEM((SPAN, heads, tok, tok), F32),
            pltpu.VMEM((SPAN, heads, tok, tok), F32),
            pltpu.VMEM((heads, SPAN, tok, tok), BF16),
            pltpu.VMEM((heads, SPAN, tok, tok), BF16),
            pltpu.VMEM(row, F32),
            pltpu.VMEM(row, F32),
            pltpu.VMEM(row, F32),
            pltpu.VMEM((SPAN,) + row, F32),
            pltpu.VMEM((tok, dim), BF16),
            pltpu.VMEM((tok, dim), BF16),
            pltpu.VMEM((tok, dim), F32),
            pltpu.VMEM((tok, dim), F32),
            pltpu.VMEM((SPAN - 1, tok, dim), BF16),
            pltpu.VMEM((SPAN - 1, tok, dim), BF16),
            pltpu.VMEM((SPAN - 1, tok, dim), BF16),
            pltpu.VMEM((SPAN - 1, tok, dim), BF16),
            pltpu.VMEM((tok, width), BF16),
            pltpu.VMEM((tok, width), BF16),
            pltpu.VMEM((tok, dim), BF16),
            pltpu.VMEM((tok, dim), BF16),
            pltpu.SemaphoreType.DMA((3 + 2 * heads,)),
            pltpu.SemaphoreType.DMA((4,)),
            pltpu.SemaphoreType.DMA((14,)),
            pltpu.SemaphoreType.DMA((14,)),
        ],
        compiler_params=pltpu.CompilerParams(
            collective_id=0, has_side_effects=True, vmem_limit_bytes=VMEM_BYTES
        ),
        cost_estimate=pl.CostEstimate(
            flops=12 * tok * heads * SPAN * tok * dim,
            bytes_accessed=8 * tok * (width + dim),
            transcendentals=SPAN * tok * tok * heads,
        ),
    )(*in_hbm)
    return pl.pallas_call(
        write_out,
        out_shape=shapes,
        in_specs=[anywhere] * 4,
        out_specs=(anywhere,) * 4,
        scratch_shapes=[pltpu.SemaphoreType.DMA((4,))],
        compiler_params=pltpu.CompilerParams(vmem_limit_bytes=VMEM_BYTES),
    )(*results)


def solution(mesh):
    rows = P(("outer", "inner"), None)

    def program(queries, key_rows, value_rows, grad_out, doc_starts, doc_ids):
        outer_count, inner_count = mesh.shape["outer"], mesh.shape["inner"]
        dim = key_rows.shape[1]
        sizes = (
            outer_count,
            inner_count,
            key_rows.shape[0] // (outer_count * inner_count),
            queries.shape[1] // dim,
            dim,
        )
        return jax.shard_map(
            functools.partial(local, sizes),
            mesh=mesh,
            in_specs=(rows, rows, rows, rows, P(), P(("outer", "inner"))),
            out_specs=(rows, rows, rows, rows),
            check_vma=False,
        )(queries, key_rows, value_rows, grad_out, doc_starts, doc_ids)

    return program
```

```python
import functools
import math

import jax
import jax.numpy as jnp
from jax import lax
from jax.experimental import pallas as pl
from jax.experimental.pallas import tpu as pltpu
from jax.sharding import PartitionSpec as P

MESH = pl.DeviceIdType.MESH
SPAN = 4
CHUNK = 32
GROUP = 2
UNROLL = 8
MASKED = -1e30
VMEM_BYTES = 48 * 2**20
F32 = jnp.float32
BF16 = jnp.bfloat16


def dot(left, right):
    return jnp.dot(left, right, preferred_element_type=F32)


def kernel(
    sizes,
    q_in, k_in, v_in, g_in, doc_in,
    att, dq, dk, dv,
    docs, q, g, qt, gt, kw, vw, kt, vt, bias, probs, dprobs, low, grad_low, row_max, row_sum, row_dot, block_max,
    relay_k, relay_v, key_sum, value_sum, send_k, send_v, got_k, got_v,
    local_sem, send_sem, recv_sem,
):
    outer_count, inner_count, tok, heads, dim = sizes
    total = outer_count * inner_count
    score_scale = 1.0 / math.sqrt(dim)
    to_log2 = score_scale * math.log2(math.e)
    me = lax.axis_index("outer") * inner_count + lax.axis_index("inner")
    odd = lax.rem(me, 2)

    def device(offset):
        place = lax.rem(me + offset + total, total)
        return (lax.div(place, inner_count), lax.rem(place, inner_count))

    sibling = device(1 - 2 * odd)

    has_two_before = me >= 2
    has_three_before = me >= 3
    has_two_after = me + 2 < total
    has_three_after = me + 3 < total
    is_odd = odd == 1
    is_even = odd == 0

    step = lax.div(lax.rem(me, 8), 2)
    relay = device(jnp.where(step == 0, 6, -2))
    relayed_from = device(jnp.where(step == 3, -6, 2))
    relay_target = jnp.where(step == 3, -3, 5)
    has_relay_target = me + relay_target < total
    relay_source = device(jnp.where(step == 2, 3, -5))

    for age in range(1, SPAN):

        @pl.when(me < age)
        def _(age=age):
            kw[age] = jnp.zeros_like(kw[age])
            vw[age] = jnp.zeros_like(vw[age])

    @pl.when(me + 3 >= total)
    def _():
        for slot in (0, 2):
            got_k[slot] = jnp.zeros_like(got_k[slot])
            got_v[slot] = jnp.zeros_like(got_v[slot])

    barrier = pltpu.get_barrier_semaphore()

    def greet(place):
        pl.semaphore_signal(barrier, inc=1, device_id=place, device_id_type=MESH)

    greet(sibling)

    @pl.when(has_two_before)
    def _():
        greet(device(-2))

    @pl.when(is_even & has_three_before)
    def _():
        greet(relay_source)

    @pl.when(is_odd & has_relay_target)
    def _():
        greet(relayed_from)

    key_load = pltpu.make_async_copy(k_in, kw.at[0], local_sem.at[0])
    value_load = pltpu.make_async_copy(v_in, vw.at[0], local_sem.at[1])
    doc_load = pltpu.make_async_copy(doc_in, docs, local_sem.at[2])
    head_loads = []
    for head in range(heads):
        here, there = pl.ds(head * dim, dim), pl.ds(head * tok, tok)
        head_loads += [
            pltpu.make_async_copy(q_in.at[:, here], q.at[there], local_sem.at[3 + head]),
            pltpu.make_async_copy(g_in.at[:, here], g.at[there], local_sem.at[3 + heads + head]),
        ]
    for copy in [key_load, value_load, doc_load] + head_loads:
        copy.start()

    def remote(source, target, place, number):
        return pltpu.make_async_remote_copy(
            src_ref=source,
            dst_ref=target,
            send_sem=send_sem.at[number],
            recv_sem=recv_sem.at[number],
            device_id=place,
            device_id_type=MESH,
        )

    def pair(keys, values, target_slot, place, number):
        return (
            remote(keys, kw.at[target_slot], place, number),
            remote(values, vw.at[target_slot], place, number + 1),
        )

    to_next = pair(kw.at[0], vw.at[0], 2, device(2), 0)
    own_to_sibling = pair(kw.at[0], vw.at[0], 1, sibling, 2)
    passed_to_sibling = pair(kw.at[2], vw.at[2], 1, sibling, 2)
    passed_on = pair(kw.at[2], vw.at[2], 3, sibling, 4)
    relay_in = (
        remote(kw.at[0], relay_k, relay, 12),
        remote(vw.at[0], relay_v, relay, 13),
    )
    relay_out = pair(relay_k, relay_v, 3, device(relay_target), 4)
    third = (
        remote(send_k.at[0], got_k.at[0], device(2 * odd - 3), 6),
        remote(send_v.at[0], got_v.at[0], device(2 * odd - 3), 7),
    )
    first = (
        remote(send_k.at[1], got_k.at[1], sibling, 8),
        remote(send_v.at[1], got_v.at[1], sibling, 9),
    )
    second = (
        remote(send_k.at[2], got_k.at[2], device(-2), 10),
        remote(send_v.at[2], got_v.at[2], device(-2), 11),
    )

    def start(copies):
        for copy in copies:
            copy.start()

    def received(copies):
        for copy in copies:
            copy.wait_recv()

    def sent(copies):
        for copy in copies:
            copy.wait_send()

    doc_load.wait()
    first_row = (me * tok).astype(F32)
    doc_starts = jnp.broadcast_to(docs[...][None, :].astype(F32), (tok, docs.shape[0])) - first_row
    positions = lax.broadcasted_iota(jnp.int32, doc_starts.shape, 0).astype(F32)
    starts = jnp.max(
        jnp.where(doc_starts <= positions, doc_starts, -first_row), axis=1, keepdims=True
    )
    starts = jnp.broadcast_to(starts, (tok, dim)).T[:1]
    places = lax.broadcasted_iota(jnp.int32, (tok, tok), 0)
    for age in range(SPAN):
        allowed = (places - age * tok).astype(F32) >= starts
        if age == 0:
            allowed = allowed & (places <= lax.broadcasted_iota(jnp.int32, (tok, tok), 1))
        bias[age] = jnp.where(allowed, 0.0, MASKED)

    key_load.wait()
    value_load.wait()
    targets = 1 + jnp.where(has_two_after, 1, 0)
    targets += jnp.where(is_odd & has_three_after, 1, 0)
    targets += jnp.where(is_odd & has_relay_target, 1, 0)
    pl.semaphore_wait(barrier, targets)

    @pl.when(is_even)
    def _():
        start(own_to_sibling)

    @pl.when(is_odd & has_two_after)
    def _():
        start(to_next)

    @pl.when(is_odd & has_three_after)
    def _():
        start(relay_in)

    def of_head(head, count=1):
        return pl.ds(pl.multiple_of(head * tok, tok), count * tok)

    for copy in head_loads:
        copy.wait()

    @pl.loop(0, heads // UNROLL)
    def _(part):
        for offset in range(UNROLL):
            head = part * UNROLL + offset
            qt[head] = q[of_head(head)].T
            gt[head] = g[of_head(head)].T

    @pl.when(is_even & has_two_after)
    def _():
        start(to_next)

    for place in range(UNROLL):
        row_max[place][...] = jnp.full(row_max[place].shape, MASKED, F32)
        row_sum[place][...] = jnp.zeros(row_sum[place].shape, F32)
        row_dot[place][...] = jnp.zeros(row_dot[place].shape, F32)

    def folded(values, combine):
        return combine(values.reshape(-1, 8, tok), axis=0)

    def multiply(slot, part, place):
        head = part * UNROLL + place
        scores = dot(kw[slot], qt[head]) + bias[slot]
        probs[place][slot, part] = scores
        top = jnp.max(folded(scores, jnp.max), axis=0, keepdims=True)
        dprobs[place][slot, part] = dot(vw[slot], gt[head])
        return jnp.maximum(row_max[place][part], top)

    def weigh(slot, part, place, top):
        added = jnp.zeros((8, tok), F32)
        dotted = jnp.zeros((8, tok), F32)
        for row in range(0, tok, CHUNK):
            rows = slice(row, row + CHUNK)
            weights = jnp.exp2((probs[place][slot, part, rows] - top) * to_log2)
            probs[place][slot, part, rows] = weights
            added += folded(weights, jnp.sum)
            dotted += folded(weights * dprobs[place][slot, part, rows], jnp.sum)
        shrink = jnp.exp2((row_max[place][part] - top) * to_log2)
        block_max[place][slot, part] = top
        row_max[place][part] = top
        row_sum[place][part] = row_sum[place][part] * shrink + jnp.sum(added, axis=0, keepdims=True)
        row_dot[place][part] = row_dot[place][part] * shrink + jnp.sum(dotted, axis=0, keepdims=True)

    def grade(slot, part, place):
        whole = 1.0 / row_sum[place][part]
        delta = row_dot[place][part] * whole
        scale = jnp.exp2((block_max[place][slot, part] - row_max[place][part]) * to_log2) * whole
        for row in range(0, tok, CHUNK):
            rows = slice(row, row + CHUNK)
            weights = probs[place][slot, part, rows] * scale
            low[place][part, slot, rows] = weights.astype(BF16)
            grad_low[place][part, slot, rows] = (
                weights * (dprobs[place][slot, part, rows] - delta)
            ).astype(BF16)

    @pl.loop(0, SPAN)
    def _(slot):
        @pl.when(slot == 1)
        def _():
            @pl.when(is_odd & has_relay_target)
            def _():
                for arrived, onward in zip(relay_in, relay_out):
                    arrived.wait_recv()
                    onward.start()

            @pl.when(is_odd & has_two_before)
            def _():
                for arrived, onward in zip(to_next, passed_to_sibling):
                    arrived.wait_recv()
                    onward.start()

            @pl.when(is_odd | has_two_before)
            def _():
                received(own_to_sibling)

        @pl.when((slot == 2) & is_even & has_two_before)
        def _():
            received(to_next)
            start(passed_on)

        @pl.when((slot == 3) & has_three_before)
        def _():
            received(relay_out)

        @pl.loop(0, heads // UNROLL)
        def _(part):
            tops = [multiply(slot, part, 0)]
            for place in range(UNROLL):
                if place + 1 < UNROLL:
                    tops.append(multiply(slot, part, place + 1))
                weigh(slot, part, place, tops[place])

    @pl.loop(0, SPAN)
    def _(turn):
        even_slot = jnp.where(turn == 0, 1, jnp.where(turn == 1, 3, 2))
        slot = jnp.where(turn == 3, 0, jnp.where(is_odd, 3 - turn, even_slot))
        key_sum[...] = jnp.zeros_like(key_sum)
        value_sum[...] = jnp.zeros_like(value_sum)

        @pl.loop(0, heads // UNROLL)
        def _(part):
            keys, values = key_sum[...], value_sum[...]
            for place in range(GROUP):
                grade(slot, part, place)
            for first in range(0, UNROLL, GROUP):
                group = range(first, first + GROUP)
                if first + GROUP < UNROLL:
                    for place in group:
                        grade(slot, part, place + GROUP)
                side_by_side = [
                    jnp.concatenate([ref[place][part, slot] for place in group], axis=1)
                    for ref in (grad_low, low)
                ]
                rows = of_head(part * UNROLL + first, GROUP)
                keys += dot(side_by_side[0], q[rows])
                values += dot(side_by_side[1], g[rows])
            key_sum[...] = keys
            value_sum[...] = values

        @pl.when((slot == 3) & has_three_before)
        def _():
            send_k[0] = key_sum[...].astype(BF16)
            send_v[0] = value_sum[...].astype(BF16)
            start(third)

        @pl.when((slot == 1) & (is_odd | has_two_before))
        def _():
            send_k[1] = key_sum[...].astype(BF16)
            send_v[1] = value_sum[...].astype(BF16)
            start(first)

        @pl.when((slot == 2) & has_two_before)
        def _():
            @pl.when(is_odd)
            def _():
                received(first)

            @pl.when(is_even)
            def _():
                received(third)

            send_k[2] = (key_sum[...] + got_k[odd].astype(F32)).astype(BF16)
            send_v[2] = (value_sum[...] + got_v[odd].astype(F32)).astype(BF16)
            start(second)

    for slot in range(SPAN):
        columns = slice(slot * tok, (slot + 1) * tok)
        kt[:, columns] = kw[slot].T
        vt[:, columns] = vw[slot].T

    @pl.loop(0, heads // UNROLL)
    def _(part):
        for place in range(UNROLL):
            columns = pl.ds(pl.multiple_of((part * UNROLL + place) * dim, dim), dim)
            weights = low[place][part].reshape(SPAN * tok, tok)
            grads = grad_low[place][part].reshape(SPAN * tok, tok)
            att[:, columns] = dot(vt[...], weights).T.astype(BF16)
            dq[:, columns] = (dot(kt[...], grads) * score_scale).T.astype(BF16)

    @pl.when(is_even)
    def _():
        received(first)

    @pl.when(is_odd & has_three_after)
    def _():
        received(third)

    key_sum[...] += got_k[1 - odd].astype(F32)
    value_sum[...] += got_v[1 - odd].astype(F32)

    @pl.when(has_two_after)
    def _():
        received(second)

    dk[...] = ((key_sum[...] + got_k[2].astype(F32)) * score_scale).astype(BF16)
    dv[...] = (value_sum[...] + got_v[2].astype(F32)).astype(BF16)

    @pl.when(has_two_after)
    def _():
        sent(to_next)

    @pl.when(is_even | has_two_before)
    def _():
        sent(own_to_sibling)

    @pl.when(is_even & has_two_before)
    def _():
        sent(passed_on)

    @pl.when(is_odd & has_three_after)
    def _():
        sent(relay_in)

    @pl.when(is_odd & has_relay_target)
    def _():
        sent(relay_out)

    @pl.when(has_three_before)
    def _():
        sent(third)

    @pl.when(is_odd | has_two_before)
    def _():
        sent(first)

    @pl.when(has_two_before)
    def _():
        sent(second)


def write_out(*refs):
    count = (len(refs) - 1) // 2
    sems = refs[-1]
    copies = [
        pltpu.make_async_copy(refs[i], refs[count + i], sems.at[i]) for i in range(count)
    ]
    for copy in copies:
        copy.start()
    for copy in copies:
        copy.wait()


def local(sizes, queries, key_rows, value_rows, grad_out, doc_starts, doc_ids):
    outer_count, inner_count, tok, heads, dim = sizes
    width = heads * dim
    anywhere = pl.BlockSpec(memory_space=pl.ANY)
    parts = heads // UNROLL
    row = (parts, 1, tok)
    shapes = (
        jax.ShapeDtypeStruct((tok, width), BF16),
        jax.ShapeDtypeStruct((tok, width), BF16),
        jax.ShapeDtypeStruct((tok, dim), BF16),
        jax.ShapeDtypeStruct((tok, dim), BF16),
    )
    in_hbm = [
        pltpu.with_memory_space_constraint(x, pltpu.HBM)
        for x in (queries, key_rows, value_rows, grad_out, doc_starts)
    ]
    results = pl.pallas_call(
        functools.partial(kernel, sizes),
        out_shape=tuple(pltpu.VMEM(shape.shape, shape.dtype) for shape in shapes),
        in_specs=[pl.BlockSpec(memory_space=pltpu.HBM)] * 5,
        out_specs=(pl.BlockSpec(memory_space=pltpu.VMEM),) * 4,
        scratch_shapes=[
            pltpu.VMEM(doc_starts.shape, jnp.int32),
            pltpu.VMEM((heads * tok, dim), BF16),
            pltpu.VMEM((heads * tok, dim), BF16),
            pltpu.VMEM((heads, dim, tok), BF16),
            pltpu.VMEM((heads, dim, tok), BF16),
            pltpu.VMEM((SPAN, tok, dim), BF16),
            pltpu.VMEM((SPAN, tok, dim), BF16),
            pltpu.VMEM((dim, SPAN * tok), BF16),
            pltpu.VMEM((dim, SPAN * tok), BF16),
            pltpu.VMEM((SPAN, tok, tok), F32),
            [pltpu.VMEM((SPAN, parts, tok, tok), F32)] * UNROLL,
            [pltpu.VMEM((SPAN, parts, tok, tok), F32)] * UNROLL,
            [pltpu.VMEM((parts, SPAN, tok, tok), BF16)] * UNROLL,
            [pltpu.VMEM((parts, SPAN, tok, tok), BF16)] * UNROLL,
            [pltpu.VMEM(row, F32)] * UNROLL,
            [pltpu.VMEM(row, F32)] * UNROLL,
            [pltpu.VMEM(row, F32)] * UNROLL,
            [pltpu.VMEM((SPAN,) + row, F32)] * UNROLL,
            pltpu.VMEM((tok, dim), BF16),
            pltpu.VMEM((tok, dim), BF16),
            pltpu.VMEM((tok, dim), F32),
            pltpu.VMEM((tok, dim), F32),
            pltpu.VMEM((SPAN - 1, tok, dim), BF16),
            pltpu.VMEM((SPAN - 1, tok, dim), BF16),
            pltpu.VMEM((SPAN - 1, tok, dim), BF16),
            pltpu.VMEM((SPAN - 1, tok, dim), BF16),
            pltpu.SemaphoreType.DMA((3 + 2 * heads,)),
            pltpu.SemaphoreType.DMA((14,)),
            pltpu.SemaphoreType.DMA((14,)),
        ],
        compiler_params=pltpu.CompilerParams(
            collective_id=0, has_side_effects=True, vmem_limit_bytes=VMEM_BYTES
        ),
        cost_estimate=pl.CostEstimate(
            flops=12 * tok * heads * SPAN * tok * dim,
            bytes_accessed=8 * tok * (width + dim),
            transcendentals=SPAN * tok * tok * heads,
        ),
    )(*in_hbm)
    return pl.pallas_call(
        write_out,
        out_shape=shapes,
        in_specs=[anywhere] * 4,
        out_specs=(anywhere,) * 4,
        scratch_shapes=[pltpu.SemaphoreType.DMA((4,))],
        compiler_params=pltpu.CompilerParams(vmem_limit_bytes=VMEM_BYTES),
    )(*results)


def solution(mesh):
    rows = P(("outer", "inner"), None)

    def program(queries, key_rows, value_rows, grad_out, doc_starts, doc_ids):
        outer_count, inner_count = mesh.shape["outer"], mesh.shape["inner"]
        dim = key_rows.shape[1]
        sizes = (
            outer_count,
            inner_count,
            key_rows.shape[0] // (outer_count * inner_count),
            queries.shape[1] // dim,
            dim,
        )
        return jax.shard_map(
            functools.partial(local, sizes),
            mesh=mesh,
            in_specs=(rows, rows, rows, rows, P(), P(("outer", "inner"))),
            out_specs=(rows, rows, rows, rows),
            check_vma=False,
        )(queries, key_rows, value_rows, grad_out, doc_starts, doc_ids)

    return program
```

```python
import functools
import math

import jax
import jax.numpy as jnp
from jax import lax
from jax.experimental import pallas as pl
from jax.experimental.pallas import tpu as pltpu
from jax.sharding import PartitionSpec as P

MESH = pl.DeviceIdType.MESH
SPAN = 4
CHUNK = 32
GROUP = 2
UNROLL = 8
MASKED = -1e30
VMEM_BYTES = 48 * 2**20
F32 = jnp.float32
BF16 = jnp.bfloat16


def dot(left, right):
    return jnp.dot(left, right, preferred_element_type=F32)


def kernel(
    sizes,
    q_in, k_in, v_in, g_in, doc_in,
    att, dq, dk, dv,
    docs, q, g, qgt, kw, vw, kt, vt, bias, probs, dprobs, low, grad_low, row_max, row_sum, row_dot, block_max,
    relay_k, relay_v, key_sum, value_sum, send_k, send_v, got_k, got_v,
    local_sem, send_sem, recv_sem,
):
    outer_count, inner_count, tok, heads, dim = sizes
    total = outer_count * inner_count
    score_scale = 1.0 / math.sqrt(dim)
    to_log2 = score_scale * math.log2(math.e)
    me = lax.axis_index("outer") * inner_count + lax.axis_index("inner")
    odd = lax.rem(me, 2)

    def device(offset):
        place = lax.rem(me + offset + total, total)
        return (lax.div(place, inner_count), lax.rem(place, inner_count))

    sibling = device(1 - 2 * odd)

    has_two_before = me >= 2
    has_three_before = me >= 3
    has_two_after = me + 2 < total
    has_three_after = me + 3 < total
    is_odd = odd == 1
    is_even = odd == 0

    step = lax.div(lax.rem(me, 8), 2)
    relay = device(jnp.where(step == 0, 6, -2))
    relayed_from = device(jnp.where(step == 3, -6, 2))
    relay_target = jnp.where(step == 3, -3, 5)
    has_relay_target = me + relay_target < total
    relay_source = device(jnp.where(step == 2, 3, -5))

    for age in range(1, SPAN):

        @pl.when(me < age)
        def _(age=age):
            kw[age] = jnp.zeros_like(kw[age])
            vw[age] = jnp.zeros_like(vw[age])

    @pl.when(me + 3 >= total)
    def _():
        for slot in (0, 2):
            got_k[slot] = jnp.zeros_like(got_k[slot])
            got_v[slot] = jnp.zeros_like(got_v[slot])

    barrier = pltpu.get_barrier_semaphore()

    def greet(place):
        pl.semaphore_signal(barrier, inc=1, device_id=place, device_id_type=MESH)

    @pl.when(is_odd)
    def _():
        greet(sibling)

    @pl.when(has_two_before)
    def _():
        greet(device(-2))

    @pl.when(is_even & has_three_before)
    def _():
        greet(relay_source)

    @pl.when(is_odd & has_relay_target)
    def _():
        greet(relayed_from)

    key_load = pltpu.make_async_copy(k_in, kw.at[0], local_sem.at[0])
    value_load = pltpu.make_async_copy(v_in, vw.at[0], local_sem.at[1])
    doc_load = pltpu.make_async_copy(doc_in, docs, local_sem.at[2])
    head_loads = []
    for head in range(heads):
        here, there = pl.ds(head * dim, dim), pl.ds(head * tok, tok)
        head_loads += [
            pltpu.make_async_copy(q_in.at[:, here], q.at[there], local_sem.at[3 + head]),
            pltpu.make_async_copy(g_in.at[:, here], g.at[there], local_sem.at[3 + heads + head]),
        ]
    for copy in [key_load, value_load, doc_load] + head_loads:
        copy.start()

    def remote(source, target, place, number):
        return pltpu.make_async_remote_copy(
            src_ref=source,
            dst_ref=target,
            send_sem=send_sem.at[number],
            recv_sem=recv_sem.at[number],
            device_id=place,
            device_id_type=MESH,
        )

    def pair(keys, values, target_slot, place, number):
        return (
            remote(keys, kw.at[target_slot], place, number),
            remote(values, vw.at[target_slot], place, number + 1),
        )

    to_next = pair(kw.at[0], vw.at[0], 2, device(2), 0)
    own_to_sibling = pair(kw.at[0], vw.at[0], 1, sibling, 2)
    passed_to_sibling = pair(kw.at[2], vw.at[2], 1, sibling, 2)
    passed_on = pair(kw.at[2], vw.at[2], 3, sibling, 4)
    relay_in = (
        remote(kw.at[0], relay_k, relay, 12),
        remote(vw.at[0], relay_v, relay, 13),
    )
    relay_out = pair(relay_k, relay_v, 3, device(relay_target), 4)
    third = (
        remote(send_k.at[0], got_k.at[0], device(2 * odd - 3), 6),
        remote(send_v.at[0], got_v.at[0], device(2 * odd - 3), 7),
    )
    first = (
        remote(send_k.at[1], got_k.at[1], sibling, 8),
        remote(send_v.at[1], got_v.at[1], sibling, 9),
    )
    second = (
        remote(send_k.at[2], got_k.at[2], device(-2), 10),
        remote(send_v.at[2], got_v.at[2], device(-2), 11),
    )

    def start(copies):
        for copy in copies:
            copy.start()

    def received(copies):
        for copy in copies:
            copy.wait_recv()

    def sent(copies):
        for copy in copies:
            copy.wait_send()

    doc_load.wait()
    first_row = (me * tok).astype(F32)
    doc_starts = jnp.broadcast_to(docs[...][None, :].astype(F32), (tok, docs.shape[0])) - first_row
    positions = lax.broadcasted_iota(jnp.int32, doc_starts.shape, 0).astype(F32)
    starts = jnp.max(
        jnp.where(doc_starts <= positions, doc_starts, -first_row), axis=1, keepdims=True
    )
    starts = jnp.broadcast_to(starts, (tok, dim)).T[:1]
    places = lax.broadcasted_iota(jnp.int32, (tok, tok), 0)
    for age in range(SPAN):
        allowed = (places - age * tok).astype(F32) >= starts
        if age == 0:
            allowed = allowed & (places <= lax.broadcasted_iota(jnp.int32, (tok, tok), 1))
        bias[age] = jnp.where(allowed, 0.0, MASKED)

    key_load.wait()
    value_load.wait()
    targets = 1 - odd + jnp.where(has_two_after, 1, 0)
    targets += jnp.where(is_odd & has_three_after, 1, 0)
    targets += jnp.where(is_odd & has_relay_target, 1, 0)
    pl.semaphore_wait(barrier, targets)

    @pl.when(is_even)
    def _():
        start(own_to_sibling)

    @pl.when(is_odd & has_two_after)
    def _():
        start(to_next)

    @pl.when(is_odd & has_three_after)
    def _():
        start(relay_in)

    def of_head(head, count=1):
        return pl.ds(pl.multiple_of(head * tok, tok), count * tok)

    for copy in head_loads:
        copy.wait()

    @pl.loop(0, heads // UNROLL)
    def _(part):
        for offset in range(UNROLL):
            head = part * UNROLL + offset
            qgt[head, :dim] = q[of_head(head)].T
            qgt[head, dim:] = g[of_head(head)].T

    @pl.when(is_even & has_two_after)
    def _():
        start(to_next)

    for place in range(UNROLL):
        row_max[place][...] = jnp.full(row_max[place].shape, MASKED, F32)
        row_sum[place][...] = jnp.zeros(row_sum[place].shape, F32)
        row_dot[place][...] = jnp.zeros(row_dot[place].shape, F32)

    def folded(values, combine):
        return combine(values.reshape(-1, 8, tok), axis=0)

    def multiply(slot, part, place):
        head = part * UNROLL + place
        nothing = jnp.zeros((tok, dim), BF16)
        keys_over_values = jnp.concatenate(
            [
                jnp.concatenate([kw[slot], nothing], axis=1),
                jnp.concatenate([nothing, vw[slot]], axis=1),
            ],
            axis=0,
        )
        both = dot(keys_over_values, qgt[head])
        scores = both[:tok] + bias[slot]
        probs[place][slot, part] = scores
        top = jnp.max(folded(scores, jnp.max), axis=0, keepdims=True)
        dprobs[place][slot, part] = both[tok:]
        return jnp.maximum(row_max[place][part], top)

    def weigh(slot, part, place, top):
        added = jnp.zeros((8, tok), F32)
        dotted = jnp.zeros((8, tok), F32)
        for row in range(0, tok, CHUNK):
            rows = slice(row, row + CHUNK)
            weights = jnp.exp2((probs[place][slot, part, rows] - top) * to_log2)
            probs[place][slot, part, rows] = weights
            added += folded(weights, jnp.sum)
            dotted += folded(weights * dprobs[place][slot, part, rows], jnp.sum)
        shrink = jnp.exp2((row_max[place][part] - top) * to_log2)
        block_max[place][slot, part] = top
        row_max[place][part] = top
        row_sum[place][part] = row_sum[place][part] * shrink + jnp.sum(added, axis=0, keepdims=True)
        row_dot[place][part] = row_dot[place][part] * shrink + jnp.sum(dotted, axis=0, keepdims=True)

    def grade(slot, part, place):
        whole = 1.0 / row_sum[place][part]
        delta = row_dot[place][part] * whole
        scale = jnp.exp2((block_max[place][slot, part] - row_max[place][part]) * to_log2) * whole
        for row in range(0, tok, CHUNK):
            rows = slice(row, row + CHUNK)
            weights = probs[place][slot, part, rows] * scale
            low[place][part, slot, rows] = weights.astype(BF16)
            grad_low[place][part, slot, rows] = (
                weights * (dprobs[place][slot, part, rows] - delta)
            ).astype(BF16)

    @pl.loop(0, SPAN)
    def _(slot):
        @pl.when(slot == 1)
        def _():
            @pl.when(is_odd & has_relay_target)
            def _():
                for arrived, onward in zip(relay_in, relay_out):
                    arrived.wait_recv()
                    onward.start()

            @pl.when(is_odd)
            def _():
                received(own_to_sibling)

                @pl.when(has_two_before)
                def _():
                    for arrived, onward in zip(to_next, passed_to_sibling):
                        arrived.wait_recv()
                        onward.start()

            @pl.when(is_even & has_two_before)
            def _():
                received(own_to_sibling)

        @pl.when((slot == 2) & is_even & has_two_before)
        def _():
            received(to_next)
            start(passed_on)

        @pl.when((slot == 3) & has_three_before)
        def _():
            received(relay_out)

        @pl.loop(0, heads // UNROLL)
        def _(part):
            tops = [multiply(slot, part, 0)]
            for place in range(UNROLL):
                if place + 1 < UNROLL:
                    tops.append(multiply(slot, part, place + 1))
                weigh(slot, part, place, tops[place])

    @pl.loop(0, SPAN)
    def _(turn):
        even_slot = jnp.where(turn == 0, 1, jnp.where(turn == 1, 3, 2))
        slot = jnp.where(turn == 3, 0, jnp.where(is_odd, 3 - turn, even_slot))
        key_sum[...] = jnp.zeros_like(key_sum)
        value_sum[...] = jnp.zeros_like(value_sum)

        @pl.loop(0, heads // UNROLL)
        def _(part):
            keys, values = key_sum[...], value_sum[...]
            for place in range(GROUP):
                grade(slot, part, place)
            for first in range(0, UNROLL, GROUP):
                group = range(first, first + GROUP)
                if first + GROUP < UNROLL:
                    for place in group:
                        grade(slot, part, place + GROUP)
                grads_over_weights = jnp.concatenate(
                    [
                        jnp.concatenate([ref[place][part, slot] for place in group], axis=1)
                        for ref in (grad_low, low)
                    ],
                    axis=0,
                )
                rows = of_head(part * UNROLL + first, GROUP)
                both = dot(grads_over_weights, jnp.concatenate([q[rows], g[rows]], axis=1))
                keys += both[:tok, :dim]
                values += both[tok:, dim:]
            key_sum[...] = keys
            value_sum[...] = values

        @pl.when((slot == 3) & has_three_before)
        def _():
            send_k[0] = key_sum[...].astype(BF16)
            send_v[0] = value_sum[...].astype(BF16)
            start(third)

        @pl.when((slot == 1) & (is_odd | has_two_before))
        def _():
            send_k[1] = key_sum[...].astype(BF16)
            send_v[1] = value_sum[...].astype(BF16)
            start(first)

        @pl.when((slot == 2) & has_two_before)
        def _():
            @pl.when(is_odd)
            def _():
                received(first)

            @pl.when(is_even)
            def _():
                received(third)

            send_k[2] = (key_sum[...] + got_k[odd].astype(F32)).astype(BF16)
            send_v[2] = (value_sum[...] + got_v[odd].astype(F32)).astype(BF16)
            start(second)

    for slot in range(SPAN):
        columns = slice(slot * tok, (slot + 1) * tok)
        kt[:, columns] = kw[slot].T
        vt[:, columns] = vw[slot].T

    @pl.loop(0, heads // UNROLL)
    def _(part):
        for place in range(UNROLL):
            columns = pl.ds(pl.multiple_of((part * UNROLL + place) * dim, dim), dim)
            weights = low[place][part].reshape(SPAN * tok, tok)
            grads = grad_low[place][part].reshape(SPAN * tok, tok)
            att[:, columns] = dot(vt[...], weights).T.astype(BF16)
            dq[:, columns] = (dot(kt[...], grads) * score_scale).T.astype(BF16)

    @pl.when(is_even)
    def _():
        received(first)

    @pl.when(is_odd & has_three_after)
    def _():
        received(third)

    key_sum[...] += got_k[1 - odd].astype(F32)
    value_sum[...] += got_v[1 - odd].astype(F32)

    @pl.when(has_two_after)
    def _():
        received(second)

    dk[...] = ((key_sum[...] + got_k[2].astype(F32)) * score_scale).astype(BF16)
    dv[...] = (value_sum[...] + got_v[2].astype(F32)).astype(BF16)

    @pl.when(has_two_after)
    def _():
        sent(to_next)

    @pl.when(is_even | has_two_before)
    def _():
        sent(own_to_sibling)

    @pl.when(is_even & has_two_before)
    def _():
        sent(passed_on)

    @pl.when(is_odd & has_three_after)
    def _():
        sent(relay_in)

    @pl.when(is_odd & has_relay_target)
    def _():
        sent(relay_out)

    @pl.when(has_three_before)
    def _():
        sent(third)

    @pl.when(is_odd | has_two_before)
    def _():
        sent(first)

    @pl.when(has_two_before)
    def _():
        sent(second)


def write_out(*refs):
    count = (len(refs) - 1) // 2
    sems = refs[-1]
    copies = [
        pltpu.make_async_copy(refs[i], refs[count + i], sems.at[i]) for i in range(count)
    ]
    for copy in copies:
        copy.start()
    for copy in copies:
        copy.wait()


def local(sizes, queries, key_rows, value_rows, grad_out, doc_starts, doc_ids):
    outer_count, inner_count, tok, heads, dim = sizes
    width = heads * dim
    anywhere = pl.BlockSpec(memory_space=pl.ANY)
    parts = heads // UNROLL
    row = (parts, 1, tok)
    shapes = (
        jax.ShapeDtypeStruct((tok, width), BF16),
        jax.ShapeDtypeStruct((tok, width), BF16),
        jax.ShapeDtypeStruct((tok, dim), BF16),
        jax.ShapeDtypeStruct((tok, dim), BF16),
    )
    in_hbm = [
        pltpu.with_memory_space_constraint(x, pltpu.HBM)
        for x in (queries, key_rows, value_rows, grad_out, doc_starts)
    ]
    results = pl.pallas_call(
        functools.partial(kernel, sizes),
        out_shape=tuple(pltpu.VMEM(shape.shape, shape.dtype) for shape in shapes),
        in_specs=[pl.BlockSpec(memory_space=pltpu.HBM)] * 5,
        out_specs=(pl.BlockSpec(memory_space=pltpu.VMEM),) * 4,
        scratch_shapes=[
            pltpu.VMEM(doc_starts.shape, jnp.int32),
            pltpu.VMEM((heads * tok, dim), BF16),
            pltpu.VMEM((heads * tok, dim), BF16),
            pltpu.VMEM((heads, 2 * dim, tok), BF16),
            pltpu.VMEM((SPAN, tok, dim), BF16),
            pltpu.VMEM((SPAN, tok, dim), BF16),
            pltpu.VMEM((dim, SPAN * tok), BF16),
            pltpu.VMEM((dim, SPAN * tok), BF16),
            pltpu.VMEM((SPAN, tok, tok), F32),
            [pltpu.VMEM((SPAN, parts, tok, tok), F32)] * UNROLL,
            [pltpu.VMEM((SPAN, parts, tok, tok), F32)] * UNROLL,
            [pltpu.VMEM((parts, SPAN, tok, tok), BF16)] * UNROLL,
            [pltpu.VMEM((parts, SPAN, tok, tok), BF16)] * UNROLL,
            [pltpu.VMEM(row, F32)] * UNROLL,
            [pltpu.VMEM(row, F32)] * UNROLL,
            [pltpu.VMEM(row, F32)] * UNROLL,
            [pltpu.VMEM((SPAN,) + row, F32)] * UNROLL,
            pltpu.VMEM((tok, dim), BF16),
            pltpu.VMEM((tok, dim), BF16),
            pltpu.VMEM((tok, dim), F32),
            pltpu.VMEM((tok, dim), F32),
            pltpu.VMEM((SPAN - 1, tok, dim), BF16),
            pltpu.VMEM((SPAN - 1, tok, dim), BF16),
            pltpu.VMEM((SPAN - 1, tok, dim), BF16),
            pltpu.VMEM((SPAN - 1, tok, dim), BF16),
            pltpu.SemaphoreType.DMA((3 + 2 * heads,)),
            pltpu.SemaphoreType.DMA((14,)),
            pltpu.SemaphoreType.DMA((14,)),
        ],
        compiler_params=pltpu.CompilerParams(
            collective_id=0, has_side_effects=True, vmem_limit_bytes=VMEM_BYTES
        ),
        cost_estimate=pl.CostEstimate(
            flops=12 * tok * heads * SPAN * tok * dim,
            bytes_accessed=8 * tok * (width + dim),
            transcendentals=SPAN * tok * tok * heads,
        ),
    )(*in_hbm)
    return pl.pallas_call(
        write_out,
        out_shape=shapes,
        in_specs=[anywhere] * 4,
        out_specs=(anywhere,) * 4,
        scratch_shapes=[pltpu.SemaphoreType.DMA((4,))],
        compiler_params=pltpu.CompilerParams(vmem_limit_bytes=VMEM_BYTES),
    )(*results)


def solution(mesh):
    rows = P(("outer", "inner"), None)

    def program(queries, key_rows, value_rows, grad_out, doc_starts, doc_ids):
        outer_count, inner_count = mesh.shape["outer"], mesh.shape["inner"]
        dim = key_rows.shape[1]
        sizes = (
            outer_count,
            inner_count,
            key_rows.shape[0] // (outer_count * inner_count),
            queries.shape[1] // dim,
            dim,
        )
        return jax.shard_map(
            functools.partial(local, sizes),
            mesh=mesh,
            in_specs=(rows, rows, rows, rows, P(), P(("outer", "inner"))),
            out_specs=(rows, rows, rows, rows),
            check_vma=False,
        )(queries, key_rows, value_rows, grad_out, doc_starts, doc_ids)

    return program
```

```python
import functools
import math

import jax
import jax.numpy as jnp
from jax import lax
from jax.experimental import pallas as pl
from jax.experimental.pallas import tpu as pltpu
from jax.sharding import PartitionSpec as P

MESH = pl.DeviceIdType.MESH
SPAN = 4
CHUNK = 32
GROUP = 2
UNROLL = 8
MASKED = -1e30
VMEM_BYTES = 48 * 2**20
F32 = jnp.float32
BF16 = jnp.bfloat16


def dot(left, right):
    return jnp.dot(left, right, preferred_element_type=F32)


def kernel(
    sizes,
    q_in, k_in, v_in, g_in, doc_in,
    att, dq, dk, dv,
    docs, q, g, qt, gt, kw, vw, kt, vt, bias, probs, dprobs, low, grad_low, row_max, row_sum, row_dot, block_max,
    relay_k, relay_v, key_sum, value_sum, send_k, send_v, got_k, got_v,
    local_sem, send_sem, recv_sem,
):
    outer_count, inner_count, tok, heads, dim = sizes
    total = outer_count * inner_count
    score_scale = 1.0 / math.sqrt(dim)
    to_log2 = score_scale * math.log2(math.e)
    me = lax.axis_index("outer") * inner_count + lax.axis_index("inner")
    odd = lax.rem(me, 2)

    def device(offset):
        place = lax.rem(me + offset + total, total)
        return (lax.div(place, inner_count), lax.rem(place, inner_count))

    sibling = device(1 - 2 * odd)

    has_two_before = me >= 2
    has_three_before = me >= 3
    has_two_after = me + 2 < total
    has_three_after = me + 3 < total
    is_odd = odd == 1
    is_even = odd == 0

    step = lax.div(lax.rem(me, 8), 2)
    relay = device(jnp.where(step == 0, 6, -2))
    relayed_from = device(jnp.where(step == 3, -6, 2))
    relay_target = jnp.where(step == 3, -3, 5)
    has_relay_target = me + relay_target < total
    relay_source = device(jnp.where(step == 2, 3, -5))

    for age in range(1, SPAN):

        @pl.when(me < age)
        def _(age=age):
            kw[age] = jnp.zeros_like(kw[age])
            vw[age] = jnp.zeros_like(vw[age])

    @pl.when(me + 3 >= total)
    def _():
        for slot in (0, 2):
            got_k[slot] = jnp.zeros_like(got_k[slot])
            got_v[slot] = jnp.zeros_like(got_v[slot])

    barrier = pltpu.get_barrier_semaphore()

    def greet(place):
        pl.semaphore_signal(barrier, inc=1, device_id=place, device_id_type=MESH)

    @pl.when(is_odd)
    def _():
        greet(sibling)

    @pl.when(has_two_before)
    def _():
        greet(device(-2))

    @pl.when(is_even & has_three_before)
    def _():
        greet(relay_source)

    @pl.when(is_odd & has_relay_target)
    def _():
        greet(relayed_from)

    key_load = pltpu.make_async_copy(k_in, kw.at[0], local_sem.at[0])
    value_load = pltpu.make_async_copy(v_in, vw.at[0], local_sem.at[1])
    doc_load = pltpu.make_async_copy(doc_in, docs, local_sem.at[2])
    head_loads = []
    for head in range(heads):
        here, there = pl.ds(head * dim, dim), pl.ds(head * tok, tok)
        head_loads += [
            pltpu.make_async_copy(q_in.at[:, here], q.at[there], local_sem.at[3 + head]),
            pltpu.make_async_copy(g_in.at[:, here], g.at[there], local_sem.at[3 + heads + head]),
        ]
    for copy in [key_load, value_load, doc_load] + head_loads:
        copy.start()

    def remote(source, target, place, number):
        return pltpu.make_async_remote_copy(
            src_ref=source,
            dst_ref=target,
            send_sem=send_sem.at[number],
            recv_sem=recv_sem.at[number],
            device_id=place,
            device_id_type=MESH,
        )

    def pair(keys, values, target_slot, place, number):
        return (
            remote(keys, kw.at[target_slot], place, number),
            remote(values, vw.at[target_slot], place, number + 1),
        )

    to_next = pair(kw.at[0], vw.at[0], 2, device(2), 0)
    own_to_sibling = pair(kw.at[0], vw.at[0], 1, sibling, 2)
    passed_to_sibling = pair(kw.at[2], vw.at[2], 1, sibling, 2)
    passed_on = pair(kw.at[2], vw.at[2], 3, sibling, 4)
    relay_in = (
        remote(kw.at[0], relay_k, relay, 12),
        remote(vw.at[0], relay_v, relay, 13),
    )
    relay_out = pair(relay_k, relay_v, 3, device(relay_target), 4)
    third = (
        remote(send_k.at[0], got_k.at[0], device(2 * odd - 3), 6),
        remote(send_v.at[0], got_v.at[0], device(2 * odd - 3), 7),
    )
    first = (
        remote(send_k.at[1], got_k.at[1], sibling, 8),
        remote(send_v.at[1], got_v.at[1], sibling, 9),
    )
    second = (
        remote(send_k.at[2], got_k.at[2], device(-2), 10),
        remote(send_v.at[2], got_v.at[2], device(-2), 11),
    )

    def start(copies):
        for copy in copies:
            copy.start()

    def received(copies):
        for copy in copies:
            copy.wait_recv()

    def sent(copies):
        for copy in copies:
            copy.wait_send()

    doc_load.wait()
    first_row = (me * tok).astype(F32)
    doc_starts = jnp.broadcast_to(docs[...][None, :].astype(F32), (tok, docs.shape[0])) - first_row
    positions = lax.broadcasted_iota(jnp.int32, doc_starts.shape, 0).astype(F32)
    starts = jnp.max(
        jnp.where(doc_starts <= positions, doc_starts, -first_row), axis=1, keepdims=True
    )
    starts = jnp.broadcast_to(starts, (tok, dim)).T[:1]
    places = lax.broadcasted_iota(jnp.int32, (tok, tok), 0)
    for age in range(SPAN):
        allowed = (places - age * tok).astype(F32) >= starts
        if age == 0:
            allowed = allowed & (places <= lax.broadcasted_iota(jnp.int32, (tok, tok), 1))
        bias[age] = jnp.where(allowed, 0.0, MASKED)

    key_load.wait()
    value_load.wait()
    targets = 1 - odd + jnp.where(has_two_after, 1, 0)
    targets += jnp.where(is_odd & has_three_after, 1, 0)
    targets += jnp.where(is_odd & has_relay_target, 1, 0)
    pl.semaphore_wait(barrier, targets)

    @pl.when(is_even)
    def _():
        start(own_to_sibling)

    @pl.when(is_odd & has_two_after)
    def _():
        start(to_next)

    @pl.when(is_odd & has_three_after)
    def _():
        start(relay_in)

    def of_head(head, count=1):
        return pl.ds(pl.multiple_of(head * tok, tok), count * tok)

    for copy in head_loads:
        copy.wait()

    @pl.loop(0, heads // UNROLL)
    def _(part):
        for offset in range(UNROLL):
            head = part * UNROLL + offset
            qt[head] = q[of_head(head)].T
            gt[head] = g[of_head(head)].T

    @pl.when(is_even & has_two_after)
    def _():
        start(to_next)

    for place in range(UNROLL):
        row_max[place][...] = jnp.full(row_max[place].shape, MASKED, F32)
        row_sum[place][...] = jnp.zeros(row_sum[place].shape, F32)
        row_dot[place][...] = jnp.zeros(row_dot[place].shape, F32)

    def folded(values, combine):
        return combine(values.reshape(-1, 8, tok), axis=0)

    def multiply(slot, part, place):
        head = part * UNROLL + place
        scores = dot(kw[slot], qt[head]) + bias[slot]
        probs[place][slot, part] = scores
        top = jnp.max(folded(scores, jnp.max), axis=0, keepdims=True)
        dprobs[place][slot, part] = dot(vw[slot], gt[head])
        return jnp.maximum(row_max[place][part], top)

    def weigh(slot, part, place, top):
        added = jnp.zeros((8, tok), F32)
        dotted = jnp.zeros((8, tok), F32)
        for row in range(0, tok, CHUNK):
            rows = slice(row, row + CHUNK)
            weights = jnp.exp2((probs[place][slot, part, rows] - top) * to_log2)
            probs[place][slot, part, rows] = weights
            added += folded(weights, jnp.sum)
            dotted += folded(weights * dprobs[place][slot, part, rows], jnp.sum)
        shrink = jnp.exp2((row_max[place][part] - top) * to_log2)
        block_max[place][slot, part] = top
        row_max[place][part] = top
        row_sum[place][part] = row_sum[place][part] * shrink + jnp.sum(added, axis=0, keepdims=True)
        row_dot[place][part] = row_dot[place][part] * shrink + jnp.sum(dotted, axis=0, keepdims=True)

    def grade(slot, part, place):
        whole = 1.0 / row_sum[place][part]
        delta = row_dot[place][part] * whole
        scale = jnp.exp2((block_max[place][slot, part] - row_max[place][part]) * to_log2) * whole
        for row in range(0, tok, CHUNK):
            rows = slice(row, row + CHUNK)
            weights = probs[place][slot, part, rows] * scale
            low[place][part, slot, rows] = weights.astype(BF16)
            grad_low[place][part, slot, rows] = (
                weights * (dprobs[place][slot, part, rows] - delta)
            ).astype(BF16)

    @pl.loop(0, SPAN)
    def _(slot):
        @pl.when(slot == 1)
        def _():
            @pl.when(is_odd & has_relay_target)
            def _():
                for arrived, onward in zip(relay_in, relay_out):
                    arrived.wait_recv()
                    onward.start()

            @pl.when(is_odd)
            def _():
                received(own_to_sibling)

                @pl.when(has_two_before)
                def _():
                    for arrived, onward in zip(to_next, passed_to_sibling):
                        arrived.wait_recv()
                        onward.start()

            @pl.when(is_even & has_two_before)
            def _():
                received(own_to_sibling)

        @pl.when((slot == 2) & is_even & has_two_before)
        def _():
            received(to_next)
            start(passed_on)

        @pl.when((slot == 3) & has_three_before)
        def _():
            received(relay_out)

        @pl.loop(0, heads // UNROLL)
        def _(part):
            tops = [multiply(slot, part, 0)]
            for place in range(UNROLL):
                if place + 1 < UNROLL:
                    tops.append(multiply(slot, part, place + 1))
                weigh(slot, part, place, tops[place])

    @pl.loop(0, SPAN)
    def _(turn):
        slot = jnp.where(turn == 3, 0, jnp.where(is_odd, 3 - turn, 1 + turn))
        key_sum[...] = jnp.zeros_like(key_sum)
        value_sum[...] = jnp.zeros_like(value_sum)

        @pl.loop(0, heads // UNROLL)
        def _(part):
            keys, values = key_sum[...], value_sum[...]
            for place in range(GROUP):
                grade(slot, part, place)
            for first in range(0, UNROLL, GROUP):
                group = range(first, first + GROUP)
                if first + GROUP < UNROLL:
                    for place in group:
                        grade(slot, part, place + GROUP)
                side_by_side = [
                    jnp.concatenate([ref[place][part, slot] for place in group], axis=1)
                    for ref in (grad_low, low)
                ]
                rows = of_head(part * UNROLL + first, GROUP)
                keys += dot(side_by_side[0], q[rows])
                values += dot(side_by_side[1], g[rows])
            key_sum[...] = keys
            value_sum[...] = values

        @pl.when((slot == 3) & has_three_before)
        def _():
            send_k[0] = key_sum[...].astype(BF16)
            send_v[0] = value_sum[...].astype(BF16)
            start(third)

        @pl.when((slot == 1) & (is_odd | has_two_before))
        def _():
            send_k[1] = key_sum[...].astype(BF16)
            send_v[1] = value_sum[...].astype(BF16)
            start(first)

        @pl.when((slot == 2) & has_two_before)
        def _():
            @pl.when(is_odd)
            def _():
                received(first)

            @pl.when(is_even)
            def _():
                received(third)

            send_k[2] = (key_sum[...] + got_k[odd].astype(F32)).astype(BF16)
            send_v[2] = (value_sum[...] + got_v[odd].astype(F32)).astype(BF16)
            start(second)

    for slot in range(SPAN):
        columns = slice(slot * tok, (slot + 1) * tok)
        kt[:, columns] = kw[slot].T
        vt[:, columns] = vw[slot].T

    @pl.loop(0, heads // UNROLL)
    def _(part):
        for place in range(UNROLL):
            columns = pl.ds(pl.multiple_of((part * UNROLL + place) * dim, dim), dim)
            weights = low[place][part].reshape(SPAN * tok, tok)
            grads = grad_low[place][part].reshape(SPAN * tok, tok)
            att[:, columns] = dot(vt[...], weights).astype(BF16).T
            dq[:, columns] = (dot(kt[...], grads) * score_scale).astype(BF16).T

    @pl.when(is_even)
    def _():
        received(first)

    @pl.when(is_odd & has_three_after)
    def _():
        received(third)

    key_sum[...] += got_k[1 - odd].astype(F32)
    value_sum[...] += got_v[1 - odd].astype(F32)

    @pl.when(has_two_after)
    def _():
        received(second)

    dk[...] = ((key_sum[...] + got_k[2].astype(F32)) * score_scale).astype(BF16)
    dv[...] = (value_sum[...] + got_v[2].astype(F32)).astype(BF16)

    @pl.when(has_two_after)
    def _():
        sent(to_next)

    @pl.when(is_even | has_two_before)
    def _():
        sent(own_to_sibling)

    @pl.when(is_even & has_two_before)
    def _():
        sent(passed_on)

    @pl.when(is_odd & has_three_after)
    def _():
        sent(relay_in)

    @pl.when(is_odd & has_relay_target)
    def _():
        sent(relay_out)

    @pl.when(has_three_before)
    def _():
        sent(third)

    @pl.when(is_odd | has_two_before)
    def _():
        sent(first)

    @pl.when(has_two_before)
    def _():
        sent(second)


def write_out(*refs):
    count = (len(refs) - 1) // 2
    sems = refs[-1]
    copies = [
        pltpu.make_async_copy(refs[i], refs[count + i], sems.at[i]) for i in range(count)
    ]
    for copy in copies:
        copy.start()
    for copy in copies:
        copy.wait()


def local(sizes, queries, key_rows, value_rows, grad_out, doc_starts, doc_ids):
    outer_count, inner_count, tok, heads, dim = sizes
    width = heads * dim
    anywhere = pl.BlockSpec(memory_space=pl.ANY)
    parts = heads // UNROLL
    row = (parts, 1, tok)
    shapes = (
        jax.ShapeDtypeStruct((tok, width), BF16),
        jax.ShapeDtypeStruct((tok, width), BF16),
        jax.ShapeDtypeStruct((tok, dim), BF16),
        jax.ShapeDtypeStruct((tok, dim), BF16),
    )
    in_hbm = [
        pltpu.with_memory_space_constraint(x, pltpu.HBM)
        for x in (queries, key_rows, value_rows, grad_out, doc_starts)
    ]
    results = pl.pallas_call(
        functools.partial(kernel, sizes),
        out_shape=tuple(pltpu.VMEM(shape.shape, shape.dtype) for shape in shapes),
        in_specs=[pl.BlockSpec(memory_space=pltpu.HBM)] * 5,
        out_specs=(pl.BlockSpec(memory_space=pltpu.VMEM),) * 4,
        scratch_shapes=[
            pltpu.VMEM(doc_starts.shape, jnp.int32),
            pltpu.VMEM((heads * tok, dim), BF16),
            pltpu.VMEM((heads * tok, dim), BF16),
            pltpu.VMEM((heads, dim, tok), BF16),
            pltpu.VMEM((heads, dim, tok), BF16),
            pltpu.VMEM((SPAN, tok, dim), BF16),
            pltpu.VMEM((SPAN, tok, dim), BF16),
            pltpu.VMEM((dim, SPAN * tok), BF16),
            pltpu.VMEM((dim, SPAN * tok), BF16),
            pltpu.VMEM((SPAN, tok, tok), F32),
            [pltpu.VMEM((SPAN, parts, tok, tok), F32)] * UNROLL,
            [pltpu.VMEM((SPAN, parts, tok, tok), F32)] * UNROLL,
            [pltpu.VMEM((parts, SPAN, tok, tok), BF16)] * UNROLL,
            [pltpu.VMEM((parts, SPAN, tok, tok), BF16)] * UNROLL,
            [pltpu.VMEM(row, F32)] * UNROLL,
            [pltpu.VMEM(row, F32)] * UNROLL,
            [pltpu.VMEM(row, F32)] * UNROLL,
            [pltpu.VMEM((SPAN,) + row, F32)] * UNROLL,
            pltpu.VMEM((tok, dim), BF16),
            pltpu.VMEM((tok, dim), BF16),
            pltpu.VMEM((tok, dim), F32),
            pltpu.VMEM((tok, dim), F32),
            pltpu.VMEM((SPAN - 1, tok, dim), BF16),
            pltpu.VMEM((SPAN - 1, tok, dim), BF16),
            pltpu.VMEM((SPAN - 1, tok, dim), BF16),
            pltpu.VMEM((SPAN - 1, tok, dim), BF16),
            pltpu.SemaphoreType.DMA((3 + 2 * heads,)),
            pltpu.SemaphoreType.DMA((14,)),
            pltpu.SemaphoreType.DMA((14,)),
        ],
        compiler_params=pltpu.CompilerParams(
            collective_id=0, has_side_effects=True, vmem_limit_bytes=VMEM_BYTES
        ),
        cost_estimate=pl.CostEstimate(
            flops=12 * tok * heads * SPAN * tok * dim,
            bytes_accessed=8 * tok * (width + dim),
            transcendentals=SPAN * tok * tok * heads,
        ),
    )(*in_hbm)
    return pl.pallas_call(
        write_out,
        out_shape=shapes,
        in_specs=[anywhere] * 4,
        out_specs=(anywhere,) * 4,
        scratch_shapes=[pltpu.SemaphoreType.DMA((4,))],
        compiler_params=pltpu.CompilerParams(vmem_limit_bytes=VMEM_BYTES),
    )(*results)


def solution(mesh):
    rows = P(("outer", "inner"), None)

    def program(queries, key_rows, value_rows, grad_out, doc_starts, doc_ids):
        outer_count, inner_count = mesh.shape["outer"], mesh.shape["inner"]
        dim = key_rows.shape[1]
        sizes = (
            outer_count,
            inner_count,
            key_rows.shape[0] // (outer_count * inner_count),
            queries.shape[1] // dim,
            dim,
        )
        return jax.shard_map(
            functools.partial(local, sizes),
            mesh=mesh,
            in_specs=(rows, rows, rows, rows, P(), P(("outer", "inner"))),
            out_specs=(rows, rows, rows, rows),
            check_vma=False,
        )(queries, key_rows, value_rows, grad_out, doc_starts, doc_ids)

    return program
```

```python
import functools
import math

import jax
import jax.numpy as jnp
from jax import lax
from jax.experimental import pallas as pl
from jax.experimental.pallas import tpu as pltpu
from jax.sharding import PartitionSpec as P

MESH = pl.DeviceIdType.MESH
SPAN = 4
CHUNK = 32
GROUP = 2
MASKED = -1e30
VMEM_BYTES = 48 * 2**20
F32 = jnp.float32
BF16 = jnp.bfloat16


def dot(left, right):
    return jnp.dot(left, right, preferred_element_type=F32)


def kernel(
    sizes,
    q_in, k_in, v_in, g_in, doc_in,
    att, dq, dk, dv,
    docs, q, g, qt, gt, kw, vw, kt, vt, bias, probs, dprobs, low, grad_low, row_max, row_sum, row_dot, block_max,
    relay_k, relay_v, part_k, part_v, send_k, send_v, got_k, got_v,
    local_sem, send_sem, recv_sem,
):
    outer_count, inner_count, tok, heads, dim = sizes
    total = outer_count * inner_count
    score_scale = 1.0 / math.sqrt(dim)
    to_log2 = score_scale * math.log2(math.e)
    me = lax.axis_index("outer") * inner_count + lax.axis_index("inner")
    odd = lax.rem(me, 2)

    def device(offset):
        place = lax.rem(me + offset + total, total)
        return (lax.div(place, inner_count), lax.rem(place, inner_count))

    sibling = device(1 - 2 * odd)

    has_two_before = me >= 2
    has_three_before = me >= 3
    has_two_after = me + 2 < total
    has_three_after = me + 3 < total
    is_odd = odd == 1
    is_even = odd == 0

    step = lax.div(lax.rem(me, 8), 2)
    relay = device(jnp.where(step == 0, 6, -2))
    relayed_from = device(jnp.where(step == 3, -6, 2))
    relay_target = jnp.where(step == 3, -3, 5)
    has_relay_target = me + relay_target < total
    relay_source = device(jnp.where(step == 2, 3, -5))

    for age in range(1, SPAN):

        @pl.when(me < age)
        def _(age=age):
            kw[age] = jnp.zeros_like(kw[age])
            vw[age] = jnp.zeros_like(vw[age])

    @pl.when(me + 3 >= total)
    def _():
        for slot in (0, 2):
            got_k[slot] = jnp.zeros_like(got_k[slot])
            got_v[slot] = jnp.zeros_like(got_v[slot])

    barrier = pltpu.get_barrier_semaphore()

    def greet(place):
        pl.semaphore_signal(barrier, inc=1, device_id=place, device_id_type=MESH)

    greet(sibling)

    @pl.when(has_two_before)
    def _():
        greet(device(-2))

    @pl.when(is_even & has_three_before)
    def _():
        greet(relay_source)

    @pl.when(is_odd & has_relay_target)
    def _():
        greet(relayed_from)

    key_load = pltpu.make_async_copy(k_in, kw.at[0], local_sem.at[0])
    value_load = pltpu.make_async_copy(v_in, vw.at[0], local_sem.at[1])
    doc_load = pltpu.make_async_copy(doc_in, docs, local_sem.at[2])
    head_loads = []
    for head in range(heads):
        here, there = pl.ds(head * dim, dim), pl.ds(head * tok, tok)
        head_loads += [
            pltpu.make_async_copy(q_in.at[:, here], q.at[there], local_sem.at[3 + head]),
            pltpu.make_async_copy(g_in.at[:, here], g.at[there], local_sem.at[3 + heads + head]),
        ]
    for copy in [key_load, value_load, doc_load] + head_loads:
        copy.start()

    def remote(source, target, place, number):
        return pltpu.make_async_remote_copy(
            src_ref=source,
            dst_ref=target,
            send_sem=send_sem.at[number],
            recv_sem=recv_sem.at[number],
            device_id=place,
            device_id_type=MESH,
        )

    def pair(keys, values, target_slot, place, number):
        return (
            remote(keys, kw.at[target_slot], place, number),
            remote(values, vw.at[target_slot], place, number + 1),
        )

    to_next = pair(kw.at[0], vw.at[0], 2, device(2), 0)
    own_to_sibling = pair(kw.at[0], vw.at[0], 1, sibling, 2)
    passed_to_sibling = pair(kw.at[2], vw.at[2], 1, sibling, 2)
    passed_on = pair(kw.at[2], vw.at[2], 3, sibling, 4)
    relay_in = (
        remote(kw.at[0], relay_k, relay, 12),
        remote(vw.at[0], relay_v, relay, 13),
    )
    relay_out = pair(relay_k, relay_v, 3, device(relay_target), 4)
    third = (
        remote(send_k.at[0], got_k.at[0], device(2 * odd - 3), 6),
        remote(send_v.at[0], got_v.at[0], device(2 * odd - 3), 7),
    )
    first = (
        remote(send_k.at[1], got_k.at[1], sibling, 8),
        remote(send_v.at[1], got_v.at[1], sibling, 9),
    )
    second = (
        remote(send_k.at[2], got_k.at[2], device(-2), 10),
        remote(send_v.at[2], got_v.at[2], device(-2), 11),
    )

    def start(copies):
        for copy in copies:
            copy.start()

    def received(copies):
        for copy in copies:
            copy.wait_recv()

    def sent(copies):
        for copy in copies:
            copy.wait_send()

    doc_load.wait()
    first_row = (me * tok).astype(F32)
    doc_starts = jnp.broadcast_to(docs[...][None, :].astype(F32), (tok, docs.shape[0])) - first_row
    positions = lax.broadcasted_iota(jnp.int32, doc_starts.shape, 0).astype(F32)
    starts = jnp.max(
        jnp.where(doc_starts <= positions, doc_starts, -first_row), axis=1, keepdims=True
    )
    starts = jnp.broadcast_to(starts, (tok, dim)).T[:1]
    places = lax.broadcasted_iota(jnp.int32, (tok, tok), 0)
    for age in range(SPAN):
        allowed = (places - age * tok).astype(F32) >= starts
        if age == 0:
            allowed = allowed & (places <= lax.broadcasted_iota(jnp.int32, (tok, tok), 1))
        bias[age] = jnp.where(allowed, 0.0, MASKED)

    key_load.wait()
    value_load.wait()
    targets = 1 + jnp.where(has_two_after, 1, 0)
    targets += jnp.where(is_odd & has_three_after, 1, 0)
    targets += jnp.where(is_odd & has_relay_target, 1, 0)
    pl.semaphore_wait(barrier, targets)

    @pl.when(is_even)
    def _():
        start(own_to_sibling)

    @pl.when(is_odd & has_two_after)
    def _():
        start(to_next)

    @pl.when(is_odd & has_three_after)
    def _():
        start(relay_in)

    def of_head(head, count=1):
        return slice(head * tok, (head + count) * tok)

    for copy in head_loads:
        copy.wait()
    for head in range(heads):
        qt[head] = q[of_head(head)].T
        gt[head] = g[of_head(head)].T

    def turn(slot):
        kt[:, of_head(slot)] = kw[slot].T
        vt[:, of_head(slot)] = vw[slot].T

    def folded(values, combine):
        return combine(values.reshape(-1, 8, tok), axis=0)

    def multiply(slot, head, fresh):
        scores = dot(kw[slot], qt[head]) + bias[slot]
        probs[slot, head] = scores
        top = jnp.max(folded(scores, jnp.max), axis=0, keepdims=True)
        if not fresh:
            top = jnp.maximum(row_max[head], top)
        dprobs[slot, head] = dot(vw[slot], gt[head])
        block_max[slot, head] = top

    def weigh(slot, head, fresh):
        top = block_max[slot, head]
        added = jnp.zeros((8, tok), F32)
        dotted = jnp.zeros((8, tok), F32)
        for row in range(0, tok, CHUNK):
            rows = slice(row, row + CHUNK)
            weights = jnp.exp2((probs[slot, head, rows] - top) * to_log2)
            probs[slot, head, rows] = weights
            added += folded(weights, jnp.sum)
            dotted += folded(weights * dprobs[slot, head, rows], jnp.sum)
        added = jnp.sum(added, axis=0, keepdims=True)
        dotted = jnp.sum(dotted, axis=0, keepdims=True)
        if not fresh:
            shrink = jnp.exp2((row_max[head] - top) * to_log2)
            added += row_sum[head] * shrink
            dotted += row_dot[head] * shrink
        row_max[head] = top
        row_sum[head] = added
        row_dot[head] = dotted

    def forward(slot, fresh):
        multiply(slot, 0, fresh)
        for head in range(heads):
            if head + 1 < heads:
                multiply(slot, head + 1, fresh)
            weigh(slot, head, fresh)

    def grade(slot, head):
        whole = 1.0 / row_sum[head]
        delta = row_dot[head] * whole
        scale = jnp.exp2((block_max[slot, head] - row_max[head]) * to_log2) * whole
        for row in range(0, tok, CHUNK):
            rows = slice(row, row + CHUNK)
            there = slice(slot * tok + row, slot * tok + row + CHUNK)
            weights = probs[slot, head, rows] * scale
            low[head, there] = weights.astype(BF16)
            grad_low[head, there] = (weights * (dprobs[slot, head, rows] - delta)).astype(BF16)

    def backward(slot):
        key_sum, value_sum = None, None
        for head in range(GROUP):
            grade(slot, head)
        for first_head in range(0, heads, GROUP):
            group = range(first_head, first_head + GROUP)
            if first_head + GROUP < heads:
                for head in group:
                    grade(slot, head + GROUP)
            side_by_side = [
                jnp.concatenate([ref[head, of_head(slot)] for head in group], axis=1)
                for ref in (grad_low, low)
            ]
            key_part = dot(side_by_side[0], q[of_head(first_head, GROUP)])
            value_part = dot(side_by_side[1], g[of_head(first_head, GROUP)])
            key_sum = key_part if key_sum is None else key_sum + key_part
            value_sum = value_part if value_sum is None else value_sum + value_part
        return key_sum, value_sum

    forward(0, True)

    @pl.when(is_odd & has_relay_target)
    def _():
        for arrived, onward in zip(relay_in, relay_out):
            arrived.wait_recv()
            onward.start()

    @pl.when(is_odd & has_two_before)
    def _():
        for arrived, onward in zip(to_next, passed_to_sibling):
            arrived.wait_recv()
            onward.start()

    @pl.when(is_even & has_two_after)
    def _():
        start(to_next)

    @pl.when(is_odd | has_two_before)
    def _():
        received(own_to_sibling)

    forward(1, False)

    @pl.when(is_even & has_two_before)
    def _():
        received(to_next)
        start(passed_on)

    forward(2, False)

    @pl.when(has_three_before)
    def _():
        received(relay_out)

    forward(3, False)
    key_sum, value_sum = backward(3)
    send_k[0] = key_sum.astype(BF16)
    send_v[0] = value_sum.astype(BF16)

    @pl.when(has_three_before)
    def _():
        start(third)

    key_sum, value_sum = backward(1)
    send_k[1] = key_sum.astype(BF16)
    send_v[1] = value_sum.astype(BF16)

    @pl.when(is_odd | has_two_before)
    def _():
        start(first)

    part_k[1], part_v[1] = backward(2)

    @pl.when(has_two_before)
    def _():
        @pl.when(is_odd)
        def _():
            received(first)

        @pl.when(is_even)
        def _():
            received(third)

        send_k[2] = (part_k[1] + got_k[odd].astype(F32)).astype(BF16)
        send_v[2] = (part_v[1] + got_v[odd].astype(F32)).astype(BF16)
        start(second)

    part_k[0], part_v[0] = backward(0)
    for slot in range(SPAN):
        turn(slot)
    for head in range(heads):
        columns = slice(head * dim, (head + 1) * dim)
        att[:, columns] = dot(vt[...], low[head]).astype(BF16).T
        dq[:, columns] = (dot(kt[...], grad_low[head]) * score_scale).astype(BF16).T
    @pl.when(is_even)
    def _():
        received(first)

    @pl.when(is_odd & has_three_after)
    def _():
        received(third)

    part_k[0] += got_k[1 - odd].astype(F32)
    part_v[0] += got_v[1 - odd].astype(F32)

    @pl.when(has_two_after)
    def _():
        received(second)

    dk[...] = ((part_k[0] + got_k[2].astype(F32)) * score_scale).astype(BF16)
    dv[...] = (part_v[0] + got_v[2].astype(F32)).astype(BF16)

    @pl.when(has_two_after)
    def _():
        sent(to_next)

    @pl.when(is_even | has_two_before)
    def _():
        sent(own_to_sibling)

    @pl.when(is_even & has_two_before)
    def _():
        sent(passed_on)

    @pl.when(is_odd & has_three_after)
    def _():
        sent(relay_in)

    @pl.when(is_odd & has_relay_target)
    def _():
        sent(relay_out)

    @pl.when(has_three_before)
    def _():
        sent(third)

    @pl.when(is_odd | has_two_before)
    def _():
        sent(first)

    @pl.when(has_two_before)
    def _():
        sent(second)


def write_out(*refs):
    count = (len(refs) - 1) // 2
    sems = refs[-1]
    copies = [
        pltpu.make_async_copy(refs[i], refs[count + i], sems.at[i]) for i in range(count)
    ]
    for copy in copies:
        copy.start()
    for copy in copies:
        copy.wait()


def local(sizes, queries, key_rows, value_rows, grad_out, doc_starts, doc_ids):
    outer_count, inner_count, tok, heads, dim = sizes
    width = heads * dim
    anywhere = pl.BlockSpec(memory_space=pl.ANY)
    row = (heads, 1, tok)
    shapes = (
        jax.ShapeDtypeStruct((tok, width), BF16),
        jax.ShapeDtypeStruct((tok, width), BF16),
        jax.ShapeDtypeStruct((tok, dim), BF16),
        jax.ShapeDtypeStruct((tok, dim), BF16),
    )
    in_hbm = [
        pltpu.with_memory_space_constraint(x, pltpu.HBM)
        for x in (queries, key_rows, value_rows, grad_out, doc_starts)
    ]
    results = pl.pallas_call(
        functools.partial(kernel, sizes),
        out_shape=tuple(pltpu.VMEM(shape.shape, shape.dtype) for shape in shapes),
        in_specs=[pl.BlockSpec(memory_space=pltpu.HBM)] * 5,
        out_specs=(pl.BlockSpec(memory_space=pltpu.VMEM),) * 4,
        scratch_shapes=[
            pltpu.VMEM(doc_starts.shape, jnp.int32),
            pltpu.VMEM((heads * tok, dim), BF16),
            pltpu.VMEM((heads * tok, dim), BF16),
            pltpu.VMEM((heads, dim, tok), BF16),
            pltpu.VMEM((heads, dim, tok), BF16),
            pltpu.VMEM((SPAN, tok, dim), BF16),
            pltpu.VMEM((SPAN, tok, dim), BF16),
            pltpu.VMEM((dim, SPAN * tok), BF16),
            pltpu.VMEM((dim, SPAN * tok), BF16),
            pltpu.VMEM((SPAN, tok, tok), F32),
            pltpu.VMEM((SPAN, heads, tok, tok), F32),
            pltpu.VMEM((SPAN, heads, tok, tok), F32),
            pltpu.VMEM((heads, SPAN * tok, tok), BF16),
            pltpu.VMEM((heads, SPAN * tok, tok), BF16),
            pltpu.VMEM(row, F32),
            pltpu.VMEM(row, F32),
            pltpu.VMEM(row, F32),
            pltpu.VMEM((SPAN,) + row, F32),
            pltpu.VMEM((tok, dim), BF16),
            pltpu.VMEM((tok, dim), BF16),
            pltpu.VMEM((2, tok, dim), F32),
            pltpu.VMEM((2, tok, dim), F32),
            pltpu.VMEM((SPAN - 1, tok, dim), BF16),
            pltpu.VMEM((SPAN - 1, tok, dim), BF16),
            pltpu.VMEM((SPAN - 1, tok, dim), BF16),
            pltpu.VMEM((SPAN - 1, tok, dim), BF16),
            pltpu.SemaphoreType.DMA((3 + 2 * heads,)),
            pltpu.SemaphoreType.DMA((14,)),
            pltpu.SemaphoreType.DMA((14,)),
        ],
        compiler_params=pltpu.CompilerParams(
            collective_id=0, has_side_effects=True, vmem_limit_bytes=VMEM_BYTES
        ),
        cost_estimate=pl.CostEstimate(
            flops=12 * tok * heads * SPAN * tok * dim,
            bytes_accessed=8 * tok * (width + dim),
            transcendentals=SPAN * tok * tok * heads,
        ),
    )(*in_hbm)
    return pl.pallas_call(
        write_out,
        out_shape=shapes,
        in_specs=[anywhere] * 4,
        out_specs=(anywhere,) * 4,
        scratch_shapes=[pltpu.SemaphoreType.DMA((4,))],
        compiler_params=pltpu.CompilerParams(vmem_limit_bytes=VMEM_BYTES),
    )(*results)


def solution(mesh):
    rows = P(("outer", "inner"), None)

    def program(queries, key_rows, value_rows, grad_out, doc_starts, doc_ids):
        outer_count, inner_count = mesh.shape["outer"], mesh.shape["inner"]
        dim = key_rows.shape[1]
        sizes = (
            outer_count,
            inner_count,
            key_rows.shape[0] // (outer_count * inner_count),
            queries.shape[1] // dim,
            dim,
        )
        return jax.shard_map(
            functools.partial(local, sizes),
            mesh=mesh,
            in_specs=(rows, rows, rows, rows, P(), P(("outer", "inner"))),
            out_specs=(rows, rows, rows, rows),
            check_vma=False,
        )(queries, key_rows, value_rows, grad_out, doc_starts, doc_ids)

    return program
```
